256 devices in a mesh: dp: 64 (over z_lo, y, x), tensor: 4 (over z_hi, core).
Axes of the slice: x: 4, y: 4, z: 8 (z_hi: 2, z_lo: 4; z = z_hi * 4 + z_lo), core: 2. Of those that a mesh axis runs over, the one named last changes fastest.
Arguments:
- activations: bfloat16 [16384, 8192], P('dp', 'tensor'), may hold values from -16 to 16
- value_output_gradient: bfloat16 [16384, 1024], P('dp', 'tensor'), may hold values from -6 to 6
- value_matrix: bfloat16 [8192, 1024], P(None, 'tensor'), may hold values from -0.0625 to 0.0625
- momentum: float32 [10240, 1024], P('dp', 'tensor'), may hold values from -0.0078125 to 0.0078125
- piece_rows: int32 [64], replicated, may hold values from 1 to 160, 8192 in all
- piece_owner: int32 [64], replicated, may hold values from 0 to 63, each once
- token_counts: int32 [64], replicated, may hold values from 1 to 256, 12288 in all
Outputs:
- input_grads: bfloat16 [16384, 8192], P('dp', 'tensor')
- new_weight: bfloat16 [8192, 1024], P(None, 'tensor')
- new_momentum: float32 [10240, 1024], P('dp', 'tensor')
The draws below stay inside these ranges and needn't reach their ends.
Inputs may be any that keep to these rules, and one draw needn't show every extreme that they name: `piece_rows`: at least one piece has 160 rows; the rows of all pieces sum to 8192. `piece_owner`: each replica owns exactly one piece. `token_counts`: the counts sum to 12288; at least one replica has 256 valid tokens.
All inputs are finite; a program needn't handle non-finite values.
Results may differ from the reference program's by a relative error of at most 0.001.
Values may be sent and summed in bfloat16 or wider, within the bound.
A program may use at most 128 MiB of HBM per device.

```python
import math
import jax
import jax.numpy as jnp
import numpy as np
from jax import lax

MODEL_WIDTH = 8192
TOK_DEV = 256
VALUE_FEATURES = 1024
TOKEN_SLOTS = 16384
OWNER_ROW_LIMIT = 160
TOTAL_VALID = 12288
N_DP = 64


def raised(array, own_key, source, target, blocks, factor):
    owner, partner = [(jnp.arange(array.shape[position]) // (array.shape[position] // blocks)).reshape([-1 if axis == position else 1 for axis in range(array.ndim)]) for position in (source, target)]
    chosen = jax.random.permutation(own_key, blocks)[partner]
    strong = (owner == chosen) | (owner == (partner + blocks // 2) % blocks)
    return jnp.where(strong, factor * array, array)


def steps_of(stream_key, shape, split, smallest, largest):
    gain = 1.0
    for dim, blocks in split:
        draws = jax.random.uniform(jax.random.fold_in(jax.random.fold_in(stream_key, 6), dim), (blocks,), jnp.float32, smallest / len(split), largest / len(split))
        gain = gain * jnp.repeat(jnp.exp(draws), shape[dim] // blocks).reshape((-1,) + (1,) * (len(shape) - 1 - dim))
    return gain


def split_up(amount, total, bound, slope):
    portions = [(1 << 20) // math.isqrt(grade ** slope) + 1 for grade in range(2, amount + 1)]
    rest, counts = total - bound - (amount - 1), [1] * (amount - 1)
    while rest > 0:
        movable = [i for i in range(amount - 1) if counts[i] < bound]
        whole, remaining = sum([portions[i] for i in movable]), rest
        for i in movable:
            addition = min(bound - counts[i], max(1, remaining * portions[i] // whole), rest)
            counts[i] = counts[i] + addition
            rest = rest - addition
    return np.array([bound] + counts)


def ragged_sizes(rng, amount, total, bound, slope):
    if amount == 2:
        one = jax.random.randint(rng, (), max(1, total - bound), min(bound, total - 1) + 1)
        return jnp.stack([one, total - one])
    lengths = jnp.asarray(split_up(amount, total, bound, slope), jnp.int32)
    pairs = (amount - 1) // 2
    donor, receiver = lengths[1:1 + 2 * pairs:2], lengths[2:2 + 2 * pairs:2]
    margin = jnp.minimum(donor - 1, bound - receiver)
    shifted = jax.random.randint(jax.random.fold_in(rng, 1), (pairs,), 0, 1 << 20) % (margin + 1)
    lengths = lengths.at[1:1 + 2 * pairs:2].set(donor - shifted).at[2:2 + 2 * pairs:2].set(receiver + shifted)
    return lengths[jax.random.permutation(jax.random.fold_in(rng, 2), amount)]


def gaussian(rng, dims, deviation, bound, split=(), kind=jnp.bfloat16):
    values = deviation * jax.random.normal(rng, dims, jnp.float32)
    if split:
        values = values * steps_of(rng, dims, split, -0.22, 0.18)
    return jnp.clip(values, -bound, bound).astype(kind)


def bell_draw_with(rng, extent, spread, most, cuts, heavy, kind=jnp.bfloat16):
    entries = spread * jax.random.normal(rng, extent, jnp.float32)
    if cuts:
        entries = entries * steps_of(rng, extent, cuts, -0.22, 0.18)
    return jnp.clip(raised(entries, jax.random.fold_in(rng, 3), *heavy), -most, most).astype(kind)


def setup_inputs(seed: int = 0) -> dict:
    seeds = jax.random.split(jax.random.key(seed), 8)
    activations = bell_draw_with(seeds[0], (TOKEN_SLOTS, MODEL_WIDTH), 1.0, 16.0, ((0, 64), (1, 4)), (0, 1, 64, 4.0))
    value_output_gradient = gaussian(seeds[1], (TOKEN_SLOTS, VALUE_FEATURES), 1.0, 6.0, ((0, 64), (1, 4)))
    value_matrix = gaussian(seeds[2], (MODEL_WIDTH, VALUE_FEATURES), MODEL_WIDTH ** -0.5, 0.0625, ((1, 4),))
    momentum = gaussian(seeds[3], (N_DP * OWNER_ROW_LIMIT, VALUE_FEATURES), 0.0005, 0.0078125, ((0, 64), (1, 4)), jnp.float32)
    piece_rows = ragged_sizes(seeds[4], N_DP, MODEL_WIDTH, OWNER_ROW_LIMIT, 2).astype(jnp.int32)
    piece_owner = jax.random.permutation(seeds[5], N_DP).astype(jnp.int32)
    token_counts = ragged_sizes(seeds[6], N_DP, TOTAL_VALID, TOK_DEV, 2).astype(jnp.int32)
    return dict(activations=activations, value_output_gradient=value_output_gradient, value_matrix=value_matrix, momentum=momentum, piece_rows=piece_rows, piece_owner=piece_owner, token_counts=token_counts)


momentum_beta = 0.9
learn_rate = 0.004
soft_eps = 0.0005

def reference(activations, value_output_gradient, value_matrix, momentum, piece_rows, piece_owner, token_counts):
    positions = jnp.arange(TOKEN_SLOTS, dtype=jnp.int32)
    is_valid = positions % TOK_DEV < jnp.repeat(token_counts, TOK_DEV)
    masked = jnp.where(is_valid[:, None], value_output_gradient, jnp.zeros_like(value_output_gradient)).astype(jnp.bfloat16)
    input_grads = lax.dot_general(masked, value_matrix, (((1,), (1,)), ((), ())), preferred_element_type=jnp.float32).astype(jnp.bfloat16)
    valid_total = jnp.sum(token_counts).astype(jnp.float32)
    grad = lax.dot_general(activations, masked, (((0,), (0,)), ((), ())), preferred_element_type=jnp.float32) / valid_total
    starts = (jnp.cumsum(piece_rows) - piece_rows).astype(jnp.int32)
    owns_piece = piece_owner[None, :] == jnp.arange(N_DP, dtype=jnp.int32)[:, None]
    own_start = lax.optimization_barrier(jnp.sum(jnp.where(owns_piece, starts[None, :], 0), axis=1))
    own_len = lax.optimization_barrier(jnp.sum(jnp.where(owns_piece, piece_rows[None, :], 0), axis=1))
    offsets = jnp.arange(OWNER_ROW_LIMIT, dtype=jnp.int32)
    source = jnp.clip(own_start[:, None] + offsets[None, :], 0, MODEL_WIDTH - 1).reshape(-1)
    in_piece = (offsets[None, :] < own_len[:, None]).reshape(-1)
    slot_grad = jnp.where(in_piece[:, None], jnp.take(grad, source, axis=0), jnp.float32(0.0))
    new_momentum = momentum_beta * momentum + (1.0 - momentum_beta) * slot_grad
    soft_sign = new_momentum / jnp.sqrt(new_momentum * new_momentum + soft_eps * soft_eps)
    row_ids = jnp.arange(MODEL_WIDTH, dtype=jnp.int32)
    inside = (row_ids[:, None] >= starts[None, :]) & (row_ids[:, None] < starts[None, :] + piece_rows[None, :])
    slot_of_row = lax.optimization_barrier(jnp.sum(jnp.where(inside, piece_owner[None, :] * OWNER_ROW_LIMIT + row_ids[:, None] - starts[None, :], 0), axis=1))
    row_sign = jnp.take(soft_sign, slot_of_row, axis=0)
    new_weight = (value_matrix.astype(jnp.float32) - learn_rate * row_sign).astype(jnp.bfloat16)
    return (input_grads, new_weight, new_momentum)
```

```python
import jax
import jax.numpy as jnp
from jax import lax
from jax.experimental import pallas as pl
from jax.experimental.pallas import tpu as pltpu
from jax.sharding import PartitionSpec as P

momentum_beta = 0.9
learn_rate = 0.004
soft_eps = 0.0005

N = 4
REPLICAS = 64
CAP = 160
HALF = 80
TOK = 256
FEAT = 256
LANES = 128
BLOCK = 2048
TILE = 512
ROWS = 8192
MESH = pl.DeviceIdType.MESH
BF = jnp.bfloat16
F32 = jnp.float32


def exchange_kernel(
    first_ref,
    turn_ref,
    total_ref,
    acts,
    dv,
    w,
    mom,
    old,
    keep,
    es,
    new_mom,
    grads_out,
    gbuf,
    ax,
    at,
    wx,
    tb,
    sb,
    yr,
    ys,
    zr,
    ts,
    tr,
    rr,
    r2,
    ps,
    p1,
    p2,
    p3,
    eb,
    slots,
    ss,
    rs,
    ls,
):
    me = lax.axis_index("dp")
    t = lax.axis_index("tensor")
    x = lax.rem(me, 4)
    y = lax.rem(me // 4, 4)
    z = me // 16
    xs = [lax.rem(x + d, 4) for d in range(N)]
    yz = [lax.rem(y + d, 4) for d in range(N)]
    zs = [lax.rem(z + d, 4) for d in range(N)]
    t1 = t + 1 - 2 * lax.rem(t, 2)
    tt = [t, t1, lax.rem(t + 2, 4), lax.rem(t1 + 2, 4)]

    def at_x(d):
        return (me - x + xs[d], t)

    def at_y(d):
        return (me + 4 * (yz[d] - y), t)

    def at_z(d):
        return (me + 16 * (zs[d] - z), t)

    def at_t(j):
        return (me, tt[j])

    partners = [f(d) for f in (at_x, at_y, at_z, at_t) for d in range(1, N)]
    barrier = pltpu.get_barrier_semaphore()
    for p in partners:
        pl.semaphore_signal(barrier, inc=1, device_id=p, device_id_type=MESH)

    n_sem = [0]
    sent = []

    def send(src, dst, to):
        i = n_sem[0]
        n_sem[0] += 1
        c = pltpu.make_async_remote_copy(
            src_ref=src,
            dst_ref=dst,
            send_sem=ss.at[i],
            recv_sem=rs.at[i],
            device_id=to,
            device_id_type=MESH,
        )
        c.start()
        sent.append(c)
        return c

    own_block = pltpu.make_async_copy(w.at[pl.ds(BLOCK * t, BLOCK)], wx.at[t], ls.at[0])
    own_block.start()

    gbuf[0, t] = dv[...]
    pl.semaphore_wait(barrier, len(partners))

    share = pl.ds(128 * (4 * y + x), 128)
    g1 = send(gbuf.at[0, t], gbuf.at[0, t], at_t(2))
    g2a = [send(gbuf.at[0, t], gbuf.at[d, t], at_x(d)) for d in range(1, N)]
    g3 = [send(gbuf.at[0, t], gbuf.at[0, t], at_t(1))]
    acts_x = [
        send(acts.at[:, pl.ds(TILE * xs[d], TILE)], ax.at[d - 1], at_x(d)) for d in range(1, N)
    ]
    w1 = [
        send(
            w.at[pl.ds(BLOCK * tt[j] + 128 * (4 * y + x), 128)], wx.at[t, share], at_t(j)
        )
        for j in (2, 3)
    ]
    w1core = send(w.at[pl.ds(BLOCK * t1, BLOCK)], wx.at[t], at_t(1))
    at[:, :TOK] = acts[:, pl.ds(TILE * x, TILE)].T
    g1.wait_recv()
    g2b = [send(gbuf.at[0, tt[2]], gbuf.at[d, tt[2]], at_x(d)) for d in range(1, N)]
    g3.append(send(gbuf.at[0, tt[2]], gbuf.at[0, tt[2]], at_t(1)))
    w2 = []
    for c in w1:
        c.wait_recv()
    for d in range(1, N):
        for j in (2, 3):
            w2.append(send(wx.at[tt[j], share], wx.at[tt[j], share], at_x(d)))
    for d in range(1, N):
        g2a[d - 1].wait_recv()
        g3.append(send(gbuf.at[d, t], gbuf.at[d, t], at_t(1)))
    for d in range(1, N):
        acts_x[d - 1].wait_recv()
        at[:, TOK * d : TOK * (d + 1)] = ax[d - 1].T
    for d in range(1, N):
        g2b[d - 1].wait_recv()
        g3.append(send(gbuf.at[d, tt[2]], gbuf.at[d, tt[2]], at_t(1)))
    for c in w2:
        c.wait_recv()
    quarter = pl.ds(512 * y, 512)
    w3 = []
    for d in range(1, N):
        for j in (2, 3):
            w3.append(send(wx.at[tt[j], quarter], wx.at[tt[j], quarter], at_y(d)))
    for c in g3:
        c.wait_recv()

    ycopies = []
    for c in range(N):
        tile = jnp.dot(at[...], gbuf[:, c].reshape(N * TOK, FEAT), preferred_element_type=F32)
        for h in range(2):
            part = slice(LANES * h, LANES * (h + 1))
            tb[h] = tile[:, part]
            for s in range(64):
                sb[c, (s // 4) % 4, s % 4, s // 16, :, part] = tb[h, pl.ds(s, 8, stride=64), :]
        ycopies.append(
            [send(sb.at[c, yz[d]], yr.at[c, d - 1], at_y(d)) for d in range(1, N)]
        )
    zcopies = []
    for c in range(N):
        for copy in ycopies[c]:
            copy.wait_recv()
        ys[c] = (sb[c, y] + yr[c, 0]) + (yr[c, 1] + yr[c, 2])
        zcopies.append(
            [send(ys.at[c, zs[d]], zr.at[c, d - 1], at_z(d)) for d in range(1, N)]
        )
    for c in range(N):
        for copy in zcopies[c]:
            copy.wait_recv()
        ts[c] = (ys[c, z] + zr[c, 0]) + (zr[c, 1] + zr[c, 2])

    tcopies = [send(ts.at[tt[j]], tr.at[t], at_t(j)) for j in range(1, N)]
    tr[t] = ts[t]
    for c in tcopies:
        c.wait_recv()
    xcopies = [send(tr.at[:, xs[d]], rr.at[:, x], at_x(d)) for d in range(1, N)]
    rr[:, x] = tr[:, x]
    r2[:, 128:, :] = jnp.zeros((2, 8, LANES), F32)
    for c in xcopies:
        c.wait_recv()
    for a in range(N):
        for b in range(N):
            for h in range(2):
                part = slice(LANES * h, LANES * (h + 1))
                r2[h, 32 * a + 8 * b : 32 * a + 8 * b + 8, :] = rr[a, b, :, part]

    for k in range(REPLICAS):
        first = first_ref[k]
        for h in range(2):
            part = slice(LANES * h, LANES * (h + 1))
            ps[k % 4, (k // 4) % 4, k // 16, :, part] = r2[h, pl.ds(first, 4), :]
    c1 = [send(ps.at[xs[d]], p1.at[x], at_x(d)) for d in range(1, N)]
    p1[x] = ps[x]
    for c in c1:
        c.wait_recv()
    c2 = [send(p1.at[:, yz[d]], p2.at[:, y], at_y(d)) for d in range(1, N)]
    p2[:, y] = p1[:, y]
    for c in c2:
        c.wait_recv()
    c3 = [send(p2.at[:, :, zs[d]], p3.at[:, :, z], at_z(d)) for d in range(1, N)]
    p3[:, :, z] = p2[:, :, z]
    for c in c3:
        c.wait_recv()
    got = p3[...].reshape(REPLICAS, 4, FEAT)
    for q in range(3):
        for h in range(2):
            eb[q, h, :64] = got[:, q, LANES * h : LANES * (h + 1)]
            eb[q, h, 64:] = got[:, q, LANES * h : LANES * (h + 1)]
    for h in range(2):
        part = slice(LANES * h, LANES * (h + 1))
        slot_grad = jnp.concatenate(
            [eb[q, h, pl.ds(turn_ref[0], 64), :] for q in range(3)], axis=0
        )[:CAP]
        slot_grad = keep[...] * (slot_grad / total_ref[0])
        moved = momentum_beta * mom[:, part] + (1.0 - momentum_beta) * slot_grad
        new_mom[:, part] = moved
        soft_sign = moved / jnp.sqrt(moved * moved + soft_eps * soft_eps)
        slots[:, part] = (old[:, part] - learn_rate * soft_sign).astype(BF)

    own_slot = pltpu.make_async_copy(slots, es.at[z, y, x], ls.at[1])
    own_slot.start()
    ez = [send(slots, es.at[z, y, x], at_z(d)) for d in range(1, N)]
    own_slot.wait()
    for c in ez:
        c.wait_recv()
    low, high = pl.ds(0, HALF), pl.ds(HALF, HALF)
    ea = [send(es.at[:, y, x, low], es.at[:, y, x, low], at_x(d)) for d in range(1, N)]
    eb1 = [send(es.at[:, y, x, high], es.at[:, y, x, high], at_y(d)) for d in range(1, N)]
    for c in ea:
        c.wait_recv()
    ea2 = [send(es.at[:, y, :, low], es.at[:, y, :, low], at_y(d)) for d in range(1, N)]
    for c in eb1:
        c.wait_recv()
    eb2 = [send(es.at[:, :, x, high], es.at[:, :, x, high], at_x(d)) for d in range(1, N)]

    own_block.wait()
    w1core.wait_recv()
    for c in w3:
        c.wait_recv()
    for n in range(N):
        part = pl.ds(512 * n, 512)
        total = jnp.zeros((TOK, 512), F32)
        for c in range(N):
            total = total + lax.dot_general(
                gbuf[0, c],
                wx[c, part],
                (((1,), (1,)), ((), ())),
                preferred_element_type=F32,
            )
        grads_out[:, part] = total.astype(BF)
    for c in ea2 + eb2:
        c.wait_recv()
    for c in sent:
        c.wait_send()


N_COPIES = 87


def prepare_kernel(place_ref, dv, w, masked, old, keep, window, wf, sem):
    copy = pltpu.make_async_copy(
        w.at[pl.ds(pl.multiple_of(place_ref[2], 16), 176)], window, sem
    )
    copy.start()
    tokens = lax.broadcasted_iota(jnp.int32, (TOK, FEAT), 0)
    masked[...] = jnp.where(tokens < place_ref[0], dv[...], jnp.zeros((TOK, FEAT), BF))
    rows = lax.broadcasted_iota(jnp.int32, (CAP, LANES), 0)
    keep[...] = jnp.where(rows < place_ref[1], 1.0, 0.0)
    wf[:, 176:, :] = jnp.zeros((2, 160, LANES), F32)
    copy.wait()
    for h in range(2):
        part = slice(LANES * h, LANES * (h + 1))
        wf[h, :176, :] = window[:, part].astype(F32)
        old[:, part] = wf[h, pl.ds(place_ref[3], CAP), :]


def place_kernel(start_ref, owner_ref, es, out, rows):
    for p in range(REPLICAS):
        for h in range(2):
            part = slice(LANES * h, LANES * (h + 1))
            rows[h, pl.ds(start_ref[p], CAP), :] = es[owner_ref[p], :, part].astype(F32)

    @pl.loop(0, 32)
    def _(i):
        here = pl.ds(pl.multiple_of(i * 256, 256), 256)
        for h in range(2):
            out[here, LANES * h : LANES * (h + 1)] = rows[h, here, :].astype(BF)


def local(acts, dv, w, mom, piece_rows, piece_owner, token_counts):
    ids = jnp.arange(REPLICAS, dtype=jnp.int32)
    starts = jnp.sum(jnp.where(ids[None, :] < ids[:, None], piece_rows[None, :], 0), axis=1)
    owns = piece_owner[None, :] == ids[:, None]
    own_start = jnp.sum(jnp.where(owns, starts[None, :], 0), axis=1)
    own_len = jnp.sum(jnp.where(owns, piece_rows[None, :], 0), axis=1)
    total = jnp.sum(token_counts).astype(F32).reshape(1)
    me = lax.axis_index("dp")
    stripe = 16 * (me % 4) + 4 * (me // 4 % 4) + me // 16
    first = (own_start - stripe + 63) // 64
    count, length, start = [
        jnp.sum(jnp.where(ids == me, v, 0)) for v in (token_counts, own_len, own_start)
    ]
    base = jnp.minimum(start // 16 * 16, ROWS - 176)
    place = jnp.stack([count, length, base, start - base])
    turn = (start % 64).reshape(1)
    smem = pl.BlockSpec(memory_space=pltpu.SMEM)
    vmem = pl.BlockSpec(memory_space=pltpu.VMEM)
    hbm = pl.BlockSpec(memory_space=pl.ANY)
    masked, old, keep = pl.pallas_call(
        prepare_kernel,
        out_shape=(
            jax.ShapeDtypeStruct((TOK, FEAT), BF),
            jax.ShapeDtypeStruct((CAP, FEAT), F32),
            jax.ShapeDtypeStruct((CAP, LANES), F32),
        ),
        in_specs=[smem, vmem, hbm],
        out_specs=(vmem, vmem, vmem),
        scratch_shapes=[
            pltpu.VMEM((176, FEAT), BF),
            pltpu.VMEM((2, 336, LANES), F32),
            pltpu.SemaphoreType.DMA,
        ],
    )(place, dv, w)
    es, new_mom, input_grads = pl.pallas_call(
        exchange_kernel,
        out_shape=(
            jax.ShapeDtypeStruct((N, N, N, CAP, FEAT), BF),
            jax.ShapeDtypeStruct((CAP, FEAT), F32),
            jax.ShapeDtypeStruct((TOK, BLOCK), BF),
        ),
        in_specs=[smem] * 3 + [vmem, vmem, hbm, vmem, vmem, vmem],
        out_specs=(hbm, vmem, vmem),
        scratch_shapes=[
            pltpu.VMEM((N, N, TOK, FEAT), BF),
            pltpu.VMEM((N - 1, TOK, TILE), BF),
            pltpu.VMEM((TILE, N * TOK), BF),
            pltpu.VMEM((N, BLOCK, FEAT), BF),
            pltpu.VMEM((2, TILE, LANES), F32),
            pltpu.VMEM((N, N, N, N, 8, FEAT), F32),
            pltpu.VMEM((N, N - 1, N, N, 8, FEAT), F32),
            pltpu.VMEM((N, N, N, 8, FEAT), F32),
            pltpu.VMEM((N, N - 1, N, 8, FEAT), F32),
            pltpu.VMEM((N, N, 8, FEAT), F32),
            pltpu.VMEM((N, N, 8, FEAT), F32),
            pltpu.VMEM((N, N, 8, FEAT), F32),
            pltpu.VMEM((2, 136, LANES), F32),
            pltpu.VMEM((N, N, N, 4, FEAT), F32),
            pltpu.VMEM((N, N, N, 4, FEAT), F32),
            pltpu.VMEM((N, N, N, 4, FEAT), F32),
            pltpu.VMEM((N, N, N, 4, FEAT), F32),
            pltpu.VMEM((3, 2, 128, LANES), F32),
            pltpu.VMEM((CAP, FEAT), BF),
            pltpu.SemaphoreType.DMA((N_COPIES,)),
            pltpu.SemaphoreType.DMA((N_COPIES,)),
            pltpu.SemaphoreType.DMA((3,)),
        ],
        compiler_params=pltpu.CompilerParams(
            collective_id=0, has_side_effects=True, vmem_limit_bytes=48 * 2**20
        ),
    )(first, turn, total, acts, masked, w, mom, old, keep)
    new_weight = pl.pallas_call(
        place_kernel,
        out_shape=jax.ShapeDtypeStruct((ROWS, FEAT), BF),
        in_specs=[smem, smem, vmem],
        out_specs=vmem,
        scratch_shapes=[pltpu.VMEM((2, ROWS + CAP, LANES), F32)],
        compiler_params=pltpu.CompilerParams(vmem_limit_bytes=48 * 2**20),
    )(starts, piece_owner, es.reshape(REPLICAS, CAP, FEAT))
    return input_grads, new_weight, new_mom


def solution(mesh):
    return jax.shard_map(
        local,
        mesh=mesh,
        in_specs=(
            P("dp", "tensor"),
            P("dp", "tensor"),
            P(None, "tensor"),
            P("dp", "tensor"),
            P(),
            P(),
            P(),
        ),
        out_specs=(P("dp", "tensor"), P(None, "tensor"), P("dp", "tensor")),
        check_vma=False,
    )
```

```python
import jax
import jax.numpy as jnp
from jax import lax
from jax.experimental import pallas as pl
from jax.experimental.pallas import tpu as pltpu
from jax.sharding import PartitionSpec as P

momentum_beta = 0.9
learn_rate = 0.004
soft_eps = 0.0005

N = 4
REPLICAS = 64
CAP = 160
HALF = 80
TOK = 256
FEAT = 256
LANES = 128
BLOCK = 2048
TILE = 512
ROWS = 8192
MESH = pl.DeviceIdType.MESH
BF = jnp.bfloat16
F32 = jnp.float32


def exchange_kernel(
    first_ref,
    turn_ref,
    total_ref,
    acts,
    dv,
    w,
    mom,
    old,
    keep,
    es,
    new_mom,
    grads_out,
    gbuf,
    ax,
    at,
    wx,
    tb,
    sb,
    yr,
    ys,
    zr,
    ts,
    tr,
    rr,
    r2,
    ps,
    p1,
    p2,
    p3,
    eb,
    slots,
    ss,
    rs,
    ls,
):
    me = lax.axis_index("dp")
    t = lax.axis_index("tensor")
    x = lax.rem(me, 4)
    y = lax.rem(me // 4, 4)
    z = me // 16
    xs = [lax.rem(x + d, 4) for d in range(N)]
    yz = [lax.rem(y + d, 4) for d in range(N)]
    zs = [lax.rem(z + d, 4) for d in range(N)]
    h = t // 2
    a = h * x + (1 - h) * y
    b = (1 - h) * x + h * y
    as_ = [lax.rem(a + d, 4) for d in range(N)]
    bs = [lax.rem(b + d, 4) for d in range(N)]
    t1 = t + 1 - 2 * lax.rem(t, 2)
    tt = [t, t1, lax.rem(t + 2, 4), lax.rem(t1 + 2, 4)]

    def at_x(d):
        return (me - x + xs[d], t)

    def at_y(d):
        return (me + 4 * (yz[d] - y), t)

    def at_z(d):
        return (me + 16 * (zs[d] - z), t)

    def at_a(d):
        return (me + h * (xs[d] - x) + (1 - h) * 4 * (yz[d] - y), t)

    def at_b(d):
        return (me + (1 - h) * (xs[d] - x) + h * 4 * (yz[d] - y), t)

    def at_t(j):
        return (me, tt[j])

    partners = [f(d) for f in (at_x, at_y, at_z, at_t) for d in range(1, N)]
    barrier = pltpu.get_barrier_semaphore()
    for p in partners:
        pl.semaphore_signal(barrier, inc=1, device_id=p, device_id_type=MESH)

    n_sem = [0]
    sent = []

    def send(src, dst, to):
        i = n_sem[0]
        n_sem[0] += 1
        c = pltpu.make_async_remote_copy(
            src_ref=src,
            dst_ref=dst,
            send_sem=ss.at[i],
            recv_sem=rs.at[i],
            device_id=to,
            device_id_type=MESH,
        )
        c.start()
        sent.append(c)
        return c

    own_block = pltpu.make_async_copy(w.at[pl.ds(BLOCK * t, BLOCK)], wx.at[t], ls.at[0])
    own_block.start()

    gbuf[0, t] = dv[...]
    pl.semaphore_wait(barrier, len(partners))

    g1 = send(gbuf.at[0, t], gbuf.at[0, t], at_t(2))
    g2a = [send(gbuf.at[0, t], gbuf.at[d, t], at_b(d)) for d in range(1, N)]
    g3 = [send(gbuf.at[0, t], gbuf.at[0, t], at_t(1))]
    acts_x, acts_y = [], []
    for d in range(1, N):
        acts_x.append(send(acts.at[:, pl.ds(TILE * xs[d], TILE)], ax.at[0, d - 1], at_x(d)))
        acts_y.append(send(acts.at[:, pl.ds(TILE * yz[d], TILE)], ax.at[1, d - 1], at_y(d)))
    w1core = send(w.at[pl.ds(BLOCK * t1, BLOCK)], wx.at[t], at_t(1))
    at[0, :, :TOK] = acts[:, pl.ds(TILE * x, TILE)].T
    at[1, :, :TOK] = acts[:, pl.ds(TILE * y, TILE)].T
    g1.wait_recv()
    g2b = [send(gbuf.at[0, tt[2]], gbuf.at[d, tt[2]], at_a(d)) for d in range(1, N)]
    g3.append(send(gbuf.at[0, tt[2]], gbuf.at[0, tt[2]], at_t(1)))

    share_x = 64 * (4 * y + x)
    share_y = 1024 + 64 * (4 * x + y)
    w1 = [
        send(w.at[pl.ds(BLOCK * tt[j] + share, 64)], wx.at[t, pl.ds(share, 64)], at_t(j))
        for j in (2, 3)
        for share in (share_x, share_y)
    ]
    for d in range(1, N):
        g2a[d - 1].wait_recv()
        g3.append(send(gbuf.at[d, t], gbuf.at[d, t], at_t(1)))
    for d in range(1, N):
        acts_x[d - 1].wait_recv()
        at[0, :, TOK * d : TOK * (d + 1)] = ax[0, d - 1].T
        acts_y[d - 1].wait_recv()
        at[1, :, TOK * d : TOK * (d + 1)] = ax[1, d - 1].T
    for d in range(1, N):
        g2b[d - 1].wait_recv()
        g3.append(send(gbuf.at[d, tt[2]], gbuf.at[d, tt[2]], at_t(1)))
    for c in w1:
        c.wait_recv()
    w2 = []
    for d in range(1, N):
        for j in (2, 3):
            here = wx.at[tt[j], pl.ds(share_x, 64)]
            w2.append(send(here, here, at_x(d)))
            here = wx.at[tt[j], pl.ds(share_y, 64)]
            w2.append(send(here, here, at_y(d)))
    for c in g3:
        c.wait_recv()

    first_sums = [None] * N
    order = (0, 2, 1, 3)
    for c in order:
        tile = jnp.dot(
            at[c // 2], gbuf[:, c].reshape(N * TOK, FEAT), preferred_element_type=F32
        )
        for half in range(2):
            part = slice(LANES * half, LANES * (half + 1))
            tb[half] = tile[:, part]
            for s in range(64):
                sb[c, (s // 4) % 4, s % 4, s // 16, :, part] = tb[
                    half, pl.ds(s, 8, stride=64), :
                ]
        to, place = (at_y, yz) if c < 2 else (at_x, xs)
        first_sums[c] = [
            send(sb.at[c, place[d]], yr.at[c, d - 1], to(d)) for d in range(1, N)
        ]
    zcopies = [None] * N
    for c in order:
        for copy in first_sums[c]:
            copy.wait_recv()
        ys[c] = (sb[c, y if c < 2 else x] + yr[c, 0]) + (yr[c, 1] + yr[c, 2])
        zcopies[c] = [send(ys.at[c, zs[d]], zr.at[c, d - 1], at_z(d)) for d in range(1, N)]
    for c in w2:
        c.wait_recv()
    w3 = []
    quarter_y, quarter_x = pl.ds(256 * y, 256), pl.ds(1024 + 256 * x, 256)
    for d in range(1, N):
        for j in (2, 3):
            w3.append(send(wx.at[tt[j], quarter_y], wx.at[tt[j], quarter_y], at_y(d)))
            w3.append(send(wx.at[tt[j], quarter_x], wx.at[tt[j], quarter_x], at_x(d)))
    for c in order:
        for copy in zcopies[c]:
            copy.wait_recv()
        ts[c] = (ys[c, z] + zr[c, 0]) + (zr[c, 1] + zr[c, 2])

    tcopies = [send(ts.at[tt[j]], tr.at[t], at_t(j)) for j in range(1, N)]
    tr[t] = ts[t]
    for c in tcopies:
        c.wait_recv()
    xcopies = [send(tr.at[:, bs[d]], rr.at[:, b], at_b(d)) for d in range(1, N)]
    rr[:, b] = tr[:, b]
    r2[:, 128:, :] = jnp.zeros((2, 8, LANES), F32)
    for c in xcopies:
        c.wait_recv()
    for i in range(N):
        for j in range(N):
            for half in range(2):
                part = slice(LANES * half, LANES * (half + 1))
                r2[half, 32 * i + 8 * j : 32 * i + 8 * j + 8, :] = rr[i, j, :, part]

    for i in range(N):
        for j in range(N):
            for k in range(N):
                first = first_ref[16 * k + (4 - 3 * h) * j + (1 + 3 * h) * i]
                for half in range(2):
                    part = slice(LANES * half, LANES * (half + 1))
                    ps[i, j, k, :, part] = r2[half, pl.ds(first, 4), :]
    c1 = [send(ps.at[bs[d]], p1.at[b], at_b(d)) for d in range(1, N)]
    p1[b] = ps[b]
    for c in c1:
        c.wait_recv()
    c2 = [send(p1.at[:, as_[d]], p2.at[:, a], at_a(d)) for d in range(1, N)]
    p2[:, a] = p1[:, a]
    for c in c2:
        c.wait_recv()
    c3 = [send(p2.at[:, :, zs[d]], p3.at[:, :, z], at_z(d)) for d in range(1, N)]
    p3[:, :, z] = p2[:, :, z]
    for c in c3:
        c.wait_recv()
    got = p3[...].reshape(REPLICAS, 4, FEAT)
    for q in range(3):
        for half in range(2):
            part = slice(LANES * half, LANES * (half + 1))
            eb[q, half, :64] = got[:, q, part]
            eb[q, half, 64:] = got[:, q, part]
    for half in range(2):
        part = slice(LANES * half, LANES * (half + 1))
        slot_grad = jnp.concatenate(
            [eb[q, half, pl.ds(turn_ref[0], 64), :] for q in range(3)], axis=0
        )[:CAP]
        slot_grad = keep[...] * (slot_grad / total_ref[0])
        moved = momentum_beta * mom[:, part] + (1.0 - momentum_beta) * slot_grad
        new_mom[:, part] = moved
        soft_sign = moved / jnp.sqrt(moved * moved + soft_eps * soft_eps)
        slots[:, part] = (old[:, part] - learn_rate * soft_sign).astype(BF)

    own_slot = pltpu.make_async_copy(slots, es.at[z, y, x], ls.at[1])
    own_slot.start()
    ez = [send(slots, es.at[z, y, x], at_z(d)) for d in range(1, N)]
    own_slot.wait()
    for c in ez:
        c.wait_recv()
    low, high = pl.ds(0, HALF), pl.ds(HALF, HALF)
    ea = [send(es.at[:, y, x, low], es.at[:, y, x, low], at_x(d)) for d in range(1, N)]
    eb1 = [send(es.at[:, y, x, high], es.at[:, y, x, high], at_y(d)) for d in range(1, N)]
    for c in ea:
        c.wait_recv()
    ea2 = [send(es.at[:, y, :, low], es.at[:, y, :, low], at_y(d)) for d in range(1, N)]
    for c in eb1:
        c.wait_recv()
    eb2 = [send(es.at[:, :, x, high], es.at[:, :, x, high], at_x(d)) for d in range(1, N)]

    own_block.wait()
    w1core.wait_recv()
    for c in w3:
        c.wait_recv()
    for n in range(N):
        part = pl.ds(512 * n, 512)
        total = jnp.zeros((TOK, 512), F32)
        for c in range(N):
            total = total + lax.dot_general(
                gbuf[0, c],
                wx[c, part],
                (((1,), (1,)), ((), ())),
                preferred_element_type=F32,
            )
        grads_out[:, part] = total.astype(BF)
    for c in ea2 + eb2:
        c.wait_recv()
    for c in sent:
        c.wait_send()


N_COPIES = 104


def prepare_kernel(
    rows_ref,
    owner_ref,
    count_ref,
    dv,
    w,
    first_ref,
    start_ref,
    turn_ref,
    total_ref,
    masked,
    old,
    keep,
    window,
    wf,
    sem,
):
    me = lax.axis_index("dp")
    h = lax.axis_index("tensor") // 2
    x, y = lax.rem(me, 4), lax.rem(me // 4, 4)
    stripe = (16 - 12 * h) * x + (4 + 12 * h) * y + me // 16

    def step(p, carry):
        start, mine, length, total = carry
        rows, owner = rows_ref[p], owner_ref[p]
        start_ref[p] = start
        first_ref[owner] = lax.div(start - stripe + 63, 64)
        here = owner == me
        return (
            start + rows,
            jnp.where(here, start, mine),
            jnp.where(here, rows, length),
            total + count_ref[p],
        )

    zero = jnp.int32(0)
    _, start, length, total = lax.fori_loop(0, REPLICAS, step, (zero, zero, zero, zero))
    base = jnp.minimum(lax.div(start, 16) * 16, ROWS - 176)
    turn_ref[0] = lax.rem(start, 64)
    total_ref[0] = total.astype(F32)
    copy = pltpu.make_async_copy(w.at[pl.ds(pl.multiple_of(base, 16), 176)], window, sem)
    copy.start()
    tokens = lax.broadcasted_iota(jnp.int32, (TOK, FEAT), 0)
    masked[...] = jnp.where(tokens < count_ref[me], dv[...], jnp.zeros((TOK, FEAT), BF))
    rows = lax.broadcasted_iota(jnp.int32, (CAP, LANES), 0)
    keep[...] = jnp.where(rows < length, 1.0, 0.0)
    wf[:, 176:, :] = jnp.zeros((2, 160, LANES), F32)
    copy.wait()
    for half in range(2):
        part = slice(LANES * half, LANES * (half + 1))
        wf[half, :176, :] = window[:, part].astype(F32)
        old[:, part] = wf[half, pl.ds(start - base, CAP), :]


def place_kernel(start_ref, owner_ref, es, out, rows):
    for p in range(REPLICAS):
        for h in range(2):
            part = slice(LANES * h, LANES * (h + 1))
            rows[h, pl.ds(start_ref[p], CAP), :] = es[owner_ref[p], :, part].astype(F32)

    @pl.loop(0, 32)
    def _(i):
        here = pl.ds(pl.multiple_of(i * 256, 256), 256)
        for h in range(2):
            out[here, LANES * h : LANES * (h + 1)] = rows[h, here, :].astype(BF)


def local(acts, dv, w, mom, piece_rows, piece_owner, token_counts):
    smem = pl.BlockSpec(memory_space=pltpu.SMEM)
    vmem = pl.BlockSpec(memory_space=pltpu.VMEM)
    hbm = pl.BlockSpec(memory_space=pl.ANY)
    first, starts, turn, total, masked, old, keep = pl.pallas_call(
        prepare_kernel,
        out_shape=(
            jax.ShapeDtypeStruct((REPLICAS,), jnp.int32),
            jax.ShapeDtypeStruct((REPLICAS,), jnp.int32),
            jax.ShapeDtypeStruct((1,), jnp.int32),
            jax.ShapeDtypeStruct((1,), F32),
            jax.ShapeDtypeStruct((TOK, FEAT), BF),
            jax.ShapeDtypeStruct((CAP, FEAT), F32),
            jax.ShapeDtypeStruct((CAP, LANES), F32),
        ),
        in_specs=[smem, smem, smem, vmem, hbm],
        out_specs=(smem, smem, smem, smem, vmem, vmem, vmem),
        scratch_shapes=[
            pltpu.VMEM((176, FEAT), BF),
            pltpu.VMEM((2, 336, LANES), F32),
            pltpu.SemaphoreType.DMA,
        ],
    )(piece_rows, piece_owner, token_counts, dv, w)
    es, new_mom, input_grads = pl.pallas_call(
        exchange_kernel,
        out_shape=(
            jax.ShapeDtypeStruct((N, N, N, CAP, FEAT), BF),
            jax.ShapeDtypeStruct((CAP, FEAT), F32),
            jax.ShapeDtypeStruct((TOK, BLOCK), BF),
        ),
        in_specs=[smem] * 3 + [vmem, vmem, hbm, vmem, vmem, vmem],
        out_specs=(hbm, vmem, vmem),
        scratch_shapes=[
            pltpu.VMEM((N, N, TOK, FEAT), BF),
            pltpu.VMEM((2, N - 1, TOK, TILE), BF),
            pltpu.VMEM((2, TILE, N * TOK), BF),
            pltpu.VMEM((N, BLOCK, FEAT), BF),
            pltpu.VMEM((2, TILE, LANES), F32),
            pltpu.VMEM((N, N, N, N, 8, FEAT), F32),
            pltpu.VMEM((N, N - 1, N, N, 8, FEAT), F32),
            pltpu.VMEM((N, N, N, 8, FEAT), F32),
            pltpu.VMEM((N, N - 1, N, 8, FEAT), F32),
            pltpu.VMEM((N, N, 8, FEAT), F32),
            pltpu.VMEM((N, N, 8, FEAT), F32),
            pltpu.VMEM((N, N, 8, FEAT), F32),
            pltpu.VMEM((2, 136, LANES), F32),
            pltpu.VMEM((N, N, N, 4, FEAT), F32),
            pltpu.VMEM((N, N, N, 4, FEAT), F32),
            pltpu.VMEM((N, N, N, 4, FEAT), F32),
            pltpu.VMEM((N, N, N, 4, FEAT), F32),
            pltpu.VMEM((3, 2, 128, LANES), F32),
            pltpu.VMEM((CAP, FEAT), BF),
            pltpu.SemaphoreType.DMA((N_COPIES,)),
            pltpu.SemaphoreType.DMA((N_COPIES,)),
            pltpu.SemaphoreType.DMA((3,)),
        ],
        compiler_params=pltpu.CompilerParams(
            collective_id=0, has_side_effects=True, vmem_limit_bytes=48 * 2**20
        ),
    )(first, turn, total, acts, masked, w, mom, old, keep)
    new_weight = pl.pallas_call(
        place_kernel,
        out_shape=jax.ShapeDtypeStruct((ROWS, FEAT), BF),
        in_specs=[smem, smem, vmem],
        out_specs=vmem,
        scratch_shapes=[pltpu.VMEM((2, ROWS + CAP, LANES), F32)],
        compiler_params=pltpu.CompilerParams(vmem_limit_bytes=48 * 2**20),
    )(starts, piece_owner, es.reshape(REPLICAS, CAP, FEAT))
    return input_grads, new_weight, new_mom


def solution(mesh):
    return jax.shard_map(
        local,
        mesh=mesh,
        in_specs=(
            P("dp", "tensor"),
            P("dp", "tensor"),
            P(None, "tensor"),
            P("dp", "tensor"),
            P(),
            P(),
            P(),
        ),
        out_specs=(P("dp", "tensor"), P(None, "tensor"), P("dp", "tensor")),
        check_vma=False,
    )
```

```python
import jax
import jax.numpy as jnp
from jax import lax
from jax.experimental import pallas as pl
from jax.experimental.pallas import tpu as pltpu
from jax.sharding import PartitionSpec as P

momentum_beta = 0.9
learn_rate = 0.004
soft_eps = 0.0005

N = 4
REPLICAS = 64
CAP = 160
HALF = 80
TOK = 256
FEAT = 256
LANES = 128
BLOCK = 2048
TILE = 512
ROWS = 8192
MESH = pl.DeviceIdType.MESH
BF = jnp.bfloat16
F32 = jnp.float32


def exchange_kernel(
    first_ref,
    turn_ref,
    total_ref,
    acts,
    dv,
    w,
    mom_in,
    state_in,
    es,
    new_mom,
    grads_out,
    gbuf,
    ax,
    at,
    wx,
    tb,
    sb,
    yr,
    ys,
    zr,
    ts,
    tr,
    rr,
    r2,
    ps,
    p1,
    p2,
    p3,
    eb,
    slots,
    mom,
    state,
    ss,
    rs,
    ls,
):
    me = lax.axis_index("dp")
    t = lax.axis_index("tensor")
    x = lax.rem(me, 4)
    y = lax.rem(me // 4, 4)
    z = me // 16
    xs = [lax.rem(x + d, 4) for d in range(N)]
    yz = [lax.rem(y + d, 4) for d in range(N)]
    zs = [lax.rem(z + d, 4) for d in range(N)]
    h = t // 2
    a = h * x + (1 - h) * y
    b = (1 - h) * x + h * y
    as_ = [lax.rem(a + d, 4) for d in range(N)]
    bs = [lax.rem(b + d, 4) for d in range(N)]
    t1 = t + 1 - 2 * lax.rem(t, 2)
    tt = [t, t1, lax.rem(t + 2, 4), lax.rem(t1 + 2, 4)]

    def at_x(d):
        return (me - x + xs[d], t)

    def at_y(d):
        return (me + 4 * (yz[d] - y), t)

    def at_z(d):
        return (me + 16 * (zs[d] - z), t)

    def at_a(d):
        return (me + h * (xs[d] - x) + (1 - h) * 4 * (yz[d] - y), t)

    def at_b(d):
        return (me + (1 - h) * (xs[d] - x) + h * 4 * (yz[d] - y), t)

    def at_t(j):
        return (me, tt[j])

    partners = [f(d) for f in (at_x, at_y, at_z, at_t) for d in range(1, N)]
    barrier = pltpu.get_barrier_semaphore()
    for p in partners:
        pl.semaphore_signal(barrier, inc=1, device_id=p, device_id_type=MESH)

    n_sem = [0]
    sent = []

    def send(src, dst, to):
        i = n_sem[0]
        n_sem[0] += 1
        c = pltpu.make_async_remote_copy(
            src_ref=src,
            dst_ref=dst,
            send_sem=ss.at[i],
            recv_sem=rs.at[i],
            device_id=to,
            device_id_type=MESH,
        )
        c.start()
        sent.append(c)
        return c

    late = [
        pltpu.make_async_copy(src, dst, ls.at[2 + i])
        for i, (src, dst) in enumerate(((mom_in, mom), (state_in, state)))
    ]
    for copy in late:
        copy.start()
    own_block = pltpu.make_async_copy(w.at[pl.ds(BLOCK * t, BLOCK)], wx.at[t], ls.at[0])
    own_block.start()

    gbuf[0, t] = dv[...]
    pl.semaphore_wait(barrier, len(partners))

    g1 = send(gbuf.at[0, t], gbuf.at[0, t], at_t(2))
    g2a = [send(gbuf.at[0, t], gbuf.at[d, t], at_b(d)) for d in range(1, N)]
    g3 = [send(gbuf.at[0, t], gbuf.at[0, t], at_t(1))]
    acts_x, acts_y = [], []
    for d in range(1, N):
        acts_x.append(send(acts.at[:, pl.ds(TILE * xs[d], TILE)], ax.at[0, d - 1], at_x(d)))
        acts_y.append(send(acts.at[:, pl.ds(TILE * yz[d], TILE)], ax.at[1, d - 1], at_y(d)))
    w1core = send(w.at[pl.ds(BLOCK * t1, BLOCK)], wx.at[t], at_t(1))
    at[0, :, :TOK] = acts[:, pl.ds(TILE * x, TILE)].T
    at[1, :, :TOK] = acts[:, pl.ds(TILE * y, TILE)].T
    g1.wait_recv()
    g2b = [send(gbuf.at[0, tt[2]], gbuf.at[d, tt[2]], at_a(d)) for d in range(1, N)]
    g3.append(send(gbuf.at[0, tt[2]], gbuf.at[0, tt[2]], at_t(1)))

    share_x = 64 * (4 * y + x)
    share_y = 1024 + 64 * (4 * x + y)
    w1 = [
        send(w.at[pl.ds(BLOCK * tt[j] + share, 64)], wx.at[t, pl.ds(share, 64)], at_t(j))
        for j in (2, 3)
        for share in (share_x, share_y)
    ]
    for d in range(1, N):
        g2a[d - 1].wait_recv()
        g3.append(send(gbuf.at[d, t], gbuf.at[d, t], at_t(1)))
    for d in range(1, N):
        acts_x[d - 1].wait_recv()
        at[0, :, TOK * d : TOK * (d + 1)] = ax[0, d - 1].T
        acts_y[d - 1].wait_recv()
        at[1, :, TOK * d : TOK * (d + 1)] = ax[1, d - 1].T
    for d in range(1, N):
        g2b[d - 1].wait_recv()
        g3.append(send(gbuf.at[d, tt[2]], gbuf.at[d, tt[2]], at_t(1)))
    for c in w1:
        c.wait_recv()
    w2 = []
    for d in range(1, N):
        for j in (2, 3):
            here = wx.at[tt[j], pl.ds(share_x, 64)]
            w2.append(send(here, here, at_x(d)))
            here = wx.at[tt[j], pl.ds(share_y, 64)]
            w2.append(send(here, here, at_y(d)))
    for c in g3:
        c.wait_recv()

    first_sums = [None] * N
    order = (0, 2, 1, 3)
    for c in order:
        tile = jnp.dot(
            at[c // 2], gbuf[:, c].reshape(N * TOK, FEAT), preferred_element_type=F32
        )
        for half in range(2):
            part = slice(LANES * half, LANES * (half + 1))
            tb[half] = tile[:, part]
            for s in range(64):
                sb[c, (s // 4) % 4, s % 4, s // 16, :, part] = tb[
                    half, pl.ds(s, 8, stride=64), :
                ]
        to, place = (at_y, yz) if c < 2 else (at_x, xs)
        first_sums[c] = [
            send(sb.at[c, place[d]], yr.at[c, d - 1], to(d)) for d in range(1, N)
        ]
    zcopies = [None] * N
    for c in order:
        for copy in first_sums[c]:
            copy.wait_recv()
        ys[c] = (sb[c, y if c < 2 else x] + yr[c, 0]) + (yr[c, 1] + yr[c, 2])
        zcopies[c] = [send(ys.at[c, zs[d]], zr.at[c, d - 1], at_z(d)) for d in range(1, N)]
    for c in w2:
        c.wait_recv()
    w3 = []
    quarter_y, quarter_x = pl.ds(256 * y, 256), pl.ds(1024 + 256 * x, 256)
    for d in range(1, N):
        for j in (2, 3):
            w3.append(send(wx.at[tt[j], quarter_y], wx.at[tt[j], quarter_y], at_y(d)))
            w3.append(send(wx.at[tt[j], quarter_x], wx.at[tt[j], quarter_x], at_x(d)))
    for c in order:
        for copy in zcopies[c]:
            copy.wait_recv()
        ts[c] = (ys[c, z] + zr[c, 0]) + (zr[c, 1] + zr[c, 2])

    tcopies = [send(ts.at[tt[j]], tr.at[t], at_t(j)) for j in range(1, N)]
    tr[t] = ts[t]
    for c in tcopies:
        c.wait_recv()
    xcopies = [send(tr.at[:, bs[d]], rr.at[:, b], at_b(d)) for d in range(1, N)]
    rr[:, b] = tr[:, b]
    r2[:, 128:, :] = jnp.zeros((2, 8, LANES), F32)
    for c in xcopies:
        c.wait_recv()
    for i in range(N):
        for j in range(N):
            for half in range(2):
                part = slice(LANES * half, LANES * (half + 1))
                r2[half, 32 * i + 8 * j : 32 * i + 8 * j + 8, :] = rr[i, j, :, part]

    for i in range(N):
        for j in range(N):
            for k in range(N):
                first = first_ref[16 * k + (4 - 3 * h) * j + (1 + 3 * h) * i]
                for half in range(2):
                    ps[half, i, j, k] = r2[half, pl.ds(first, 4), :]
    c1 = [send(ps.at[0, bs[d]], p1.at[0, b], at_b(d)) for d in range(1, N)]
    k1 = [send(ps.at[1, :, :, zs[d]], p1.at[1, :, :, z], at_z(d)) for d in range(1, N)]
    p1[0, b] = ps[0, b]
    p1[1, :, :, z] = ps[1, :, :, z]
    for c in c1:
        c.wait_recv()
    c2 = [send(p1.at[0, :, as_[d]], p2.at[0, :, a], at_a(d)) for d in range(1, N)]
    p2[0, :, a] = p1[0, :, a]
    for c in k1:
        c.wait_recv()
    k2 = [send(p1.at[1, bs[d]], p2.at[1, b], at_b(d)) for d in range(1, N)]
    p2[1, b] = p1[1, b]
    for c in c2:
        c.wait_recv()
    c3 = [send(p2.at[0, :, :, zs[d]], p3.at[0, :, :, z], at_z(d)) for d in range(1, N)]
    p3[0, :, :, z] = p2[0, :, :, z]
    for c in k2:
        c.wait_recv()
    k3 = [send(p2.at[1, :, as_[d]], p3.at[1, :, a], at_a(d)) for d in range(1, N)]
    p3[1, :, a] = p2[1, :, a]
    for copy in late:
        copy.wait()
    for c in c3 + k3:
        c.wait_recv()
    for half in range(2):
        got = p3[half].reshape(REPLICAS, 4, LANES)
        for q in range(3):
            eb[q, half, :64] = got[:, q]
            eb[q, half, 64:] = got[:, q]
    for half in range(2):
        part = slice(LANES * half, LANES * (half + 1))
        slot_grad = jnp.concatenate(
            [eb[q, half, pl.ds(turn_ref[0], 64), :] for q in range(3)], axis=0
        )[:CAP]
        slot_grad = state[:, FEAT:] * (slot_grad / total_ref[0])
        moved = momentum_beta * mom[:, part] + (1.0 - momentum_beta) * slot_grad
        new_mom[:, part] = moved
        soft_sign = moved / jnp.sqrt(moved * moved + soft_eps * soft_eps)
        slots[:, part] = (state[:, part] - learn_rate * soft_sign).astype(BF)

    own_slot = pltpu.make_async_copy(slots, es.at[z, y, x], ls.at[1])
    own_slot.start()
    ez = [send(slots, es.at[z, y, x], at_z(d)) for d in range(1, N)]

    own_block.wait()
    w1core.wait_recv()
    for c in w3:
        c.wait_recv()
    for n in range(N):
        part = pl.ds(512 * n, 512)
        total = jnp.zeros((TOK, 512), F32)
        for c in range(N):
            total = total + lax.dot_general(
                gbuf[0, c],
                wx[c, part],
                (((1,), (1,)), ((), ())),
                preferred_element_type=F32,
            )
        grads_out[:, part] = total.astype(BF)

    own_slot.wait()
    for c in ez:
        c.wait_recv()
    low, high = pl.ds(0, HALF), pl.ds(HALF, HALF)
    near, far = pl.ds(0, 2), pl.ds(2, 2)

    def column(axis, d, zz):
        if axis == "y":
            return es.at[zz, y, lax.rem(x - d + 4, 4), low]
        return es.at[zz, lax.rem(y - d + 4, 4), x, high]

    def passed(axis, d, back, zz):
        if axis == "y":
            return es.at[zz, lax.rem(y - back + 4, 4), lax.rem(x - d + 4, 4), low]
        return es.at[zz, lax.rem(y - d + 4, 4), lax.rem(x - back + 4, 4), high]

    def spread(axis, d):
        to = at_y if axis == "y" else at_x
        out = {}
        for key, zz, step in (("up", near, 1), ("down", far, 3)):
            out[key] = send(column(axis, d, zz), column(axis, d, zz), to(step))
        for key, zz, step in (("up2", far, 1), ("down2", near, 3)):
            out[key] = send(column(axis, d, zz), column(axis, d, zz), to(step))
        return out

    def forward(axis, d, out):
        to = at_y if axis == "y" else at_x
        out["up"].wait_recv()
        here = passed(axis, d, 1, near)
        out["fup"] = send(here, here, to(1))
        out["down"].wait_recv()
        here = passed(axis, d, 3, far)
        out["fdown"] = send(here, here, to(3))

    steps = {
        axis: [
            send(own, own, to(d))
            for to in ((at_x if axis == "y" else at_y),)
            for own in (column(axis, 0, pl.ds(0, 4)),)
            for d in (1, 3, 2)
        ]
        for axis in ("y", "x")
    }
    outs = {axis: [(0, spread(axis, 0))] for axis in ("y", "x")}
    for i, d in enumerate((1, 3)):
        for axis in ("y", "x"):
            steps[axis][i].wait_recv()
            outs[axis].append((d, spread(axis, d)))
    for axis in ("y", "x"):
        forward(axis, *outs[axis][0])
    for axis in ("y", "x"):
        steps[axis][2].wait_recv()
        outs[axis].append((2, spread(axis, 2)))
    for i in (1, 2, 3):
        for axis in ("y", "x"):
            forward(axis, *outs[axis][i])
    for axis in ("y", "x"):
        for _, out in outs[axis]:
            for key in ("up2", "down2", "fup", "fdown"):
                out[key].wait_recv()
    for c in sent:
        c.wait_send()


N_COPIES = 155


def prepare_kernel(
    rows_ref,
    owner_ref,
    count_ref,
    dv,
    w,
    first_ref,
    start_ref,
    turn_ref,
    total_ref,
    masked,
    state,
    window,
    wf,
    sem,
):
    me = lax.axis_index("dp")
    h = lax.axis_index("tensor") // 2
    x, y = lax.rem(me, 4), lax.rem(me // 4, 4)
    stripe = (16 - 12 * h) * x + (4 + 12 * h) * y + me // 16

    def step(p, carry):
        start, mine, length, total = carry
        rows, owner = rows_ref[p], owner_ref[p]
        start_ref[p] = start
        first_ref[owner] = lax.div(start - stripe + 63, 64)
        here = owner == me
        return (
            start + rows,
            jnp.where(here, start, mine),
            jnp.where(here, rows, length),
            total + count_ref[p],
        )

    zero = jnp.int32(0)
    _, start, length, total = lax.fori_loop(0, REPLICAS, step, (zero, zero, zero, zero))
    base = jnp.minimum(lax.div(start, 16) * 16, ROWS - 176)
    turn_ref[0] = lax.rem(start, 64)
    total_ref[0] = total.astype(F32)
    copy = pltpu.make_async_copy(w.at[pl.ds(pl.multiple_of(base, 16), 176)], window, sem)
    copy.start()
    tokens = lax.broadcasted_iota(jnp.int32, (TOK, FEAT), 0)
    masked[...] = jnp.where(tokens < count_ref[me], dv[...], jnp.zeros((TOK, FEAT), BF))
    rows = lax.broadcasted_iota(jnp.int32, (CAP, LANES), 0)
    state[:, FEAT:] = jnp.where(rows < length, 1.0, 0.0)
    wf[:, 176:, :] = jnp.zeros((2, 160, LANES), F32)
    copy.wait()
    for half in range(2):
        part = slice(LANES * half, LANES * (half + 1))
        wf[half, :176, :] = window[:, part].astype(F32)
        state[:, part] = wf[half, pl.ds(start - base, CAP), :]


def place_kernel(start_ref, owner_ref, es, out, rows):
    for p in range(REPLICAS):
        piece = es[owner_ref[p]]
        for half in range(2):
            part = slice(LANES * half, LANES * (half + 1))
            rows[half, pl.ds(start_ref[p], CAP), :] = piece[:, part].astype(F32)

    @pl.loop(0, 32)
    def _(i):
        here = pl.ds(pl.multiple_of(i * 256, 256), 256)
        for half in range(2):
            part = slice(LANES * half, LANES * (half + 1))
            out[here, part] = rows[half, here, :].astype(BF)


def local(acts, dv, w, mom, piece_rows, piece_owner, token_counts):
    smem = pl.BlockSpec(memory_space=pltpu.SMEM)
    vmem = pl.BlockSpec(memory_space=pltpu.VMEM)
    hbm = pl.BlockSpec(memory_space=pl.ANY)
    first, starts, turn, total, masked, state = pl.pallas_call(
        prepare_kernel,
        out_shape=(
            jax.ShapeDtypeStruct((REPLICAS,), jnp.int32),
            jax.ShapeDtypeStruct((REPLICAS,), jnp.int32),
            jax.ShapeDtypeStruct((1,), jnp.int32),
            jax.ShapeDtypeStruct((1,), F32),
            jax.ShapeDtypeStruct((TOK, FEAT), BF),
            jax.ShapeDtypeStruct((CAP, FEAT + LANES), F32),
        ),
        in_specs=[smem, smem, smem, vmem, hbm],
        out_specs=(smem, smem, smem, smem, vmem, vmem),
        scratch_shapes=[
            pltpu.VMEM((176, FEAT), BF),
            pltpu.VMEM((2, 336, LANES), F32),
            pltpu.SemaphoreType.DMA,
        ],
    )(piece_rows, piece_owner, token_counts, dv, w)
    es, new_mom, input_grads = pl.pallas_call(
        exchange_kernel,
        out_shape=(
            jax.ShapeDtypeStruct((N, N, N, CAP, FEAT), BF),
            jax.ShapeDtypeStruct((CAP, FEAT), F32),
            jax.ShapeDtypeStruct((TOK, BLOCK), BF),
        ),
        in_specs=[smem] * 3 + [vmem, vmem] + [hbm] * 3,
        out_specs=(vmem, vmem, vmem),
        scratch_shapes=[
            pltpu.VMEM((N, N, TOK, FEAT), BF),
            pltpu.VMEM((2, N - 1, TOK, TILE), BF),
            pltpu.VMEM((2, TILE, N * TOK), BF),
            pltpu.VMEM((N, BLOCK, FEAT), BF),
            pltpu.VMEM((2, TILE, LANES), F32),
            pltpu.VMEM((N, N, N, N, 8, FEAT), F32),
            pltpu.VMEM((N, N - 1, N, N, 8, FEAT), F32),
            pltpu.VMEM((N, N, N, 8, FEAT), F32),
            pltpu.VMEM((N, N - 1, N, 8, FEAT), F32),
            pltpu.VMEM((N, N, 8, FEAT), F32),
            pltpu.VMEM((N, N, 8, FEAT), F32),
            pltpu.VMEM((N, N, 8, FEAT), F32),
            pltpu.VMEM((2, 136, LANES), F32),
            pltpu.VMEM((2, N, N, N, 4, LANES), F32),
            pltpu.VMEM((2, N, N, N, 4, LANES), F32),
            pltpu.VMEM((2, N, N, N, 4, LANES), F32),
            pltpu.VMEM((2, N, N, N, 4, LANES), F32),
            pltpu.VMEM((3, 2, 128, LANES), F32),
            pltpu.VMEM((CAP, FEAT), BF),
            pltpu.VMEM((CAP, FEAT), F32),
            pltpu.VMEM((CAP, FEAT + LANES), F32),
            pltpu.SemaphoreType.DMA((N_COPIES,)),
            pltpu.SemaphoreType.DMA((N_COPIES,)),
            pltpu.SemaphoreType.DMA((4,)),
        ],
        compiler_params=pltpu.CompilerParams(
            collective_id=0, has_side_effects=True, vmem_limit_bytes=32 * 2**20
        ),
    )(first, turn, total, acts, masked, w, mom, state)
    new_weight = pl.pallas_call(
        place_kernel,
        out_shape=jax.ShapeDtypeStruct((ROWS, FEAT), BF),
        in_specs=[smem, smem, vmem],
        out_specs=vmem,
        scratch_shapes=[pltpu.VMEM((2, ROWS + CAP, LANES), F32)],
        compiler_params=pltpu.CompilerParams(vmem_limit_bytes=24 * 2**20),
    )(starts, piece_owner, es.reshape(REPLICAS, CAP, FEAT))
    return input_grads, new_weight, new_mom


def solution(mesh):
    return jax.shard_map(
        local,
        mesh=mesh,
        in_specs=(
            P("dp", "tensor"),
            P("dp", "tensor"),
            P(None, "tensor"),
            P("dp", "tensor"),
            P(),
            P(),
            P(),
        ),
        out_specs=(P("dp", "tensor"), P(None, "tensor"), P("dp", "tensor")),
        check_vma=False,
    )
```

```python
import jax
import jax.numpy as jnp
from jax import lax
from jax.experimental import pallas as pl
from jax.experimental.pallas import tpu as pltpu
from jax.sharding import PartitionSpec as P

momentum_beta = 0.9
learn_rate = 0.004
soft_eps = 0.0005

N = 4
REPLICAS = 64
CAP = 160
HELD = 128
HALF = 64
TOK = 256
FEAT = 256
LANES = 128
BLOCK = 2048
TILE = 512
ROWS = 8192
MESH = pl.DeviceIdType.MESH
BF = jnp.bfloat16
F32 = jnp.float32


def exchange_kernel(
    first_ref,
    source_ref,
    turn_ref,
    total_ref,
    acts,
    dv,
    mom,
    w,
    keep_in,
    es,
    new_mom,
    grads_out,
    gbuf,
    ax,
    at,
    wx,
    tb,
    sb,
    yr,
    ys,
    zr,
    ts,
    tr,
    rr,
    r2,
    mb,
    pb,
    flat,
    held,
    eb,
    wt,
    old,
    slots,
    keep,
    ss,
    rs,
    ls,
):
    me = lax.axis_index("dp")
    t = lax.axis_index("tensor")
    x = lax.rem(me, 4)
    y = lax.rem(me // 4, 4)
    z = me // 16
    xs = [lax.rem(x + d, 4) for d in range(N)]
    yz = [lax.rem(y + d, 4) for d in range(N)]
    zs = [lax.rem(z + d, 4) for d in range(N)]
    h = t // 2
    a = h * x + (1 - h) * y
    b = (1 - h) * x + h * y
    as_ = [lax.rem(a + d, 4) for d in range(N)]
    bs = [lax.rem(b + d, 4) for d in range(N)]
    t1 = t + 1 - 2 * lax.rem(t, 2)
    tt = [t, t1, lax.rem(t + 2, 4), lax.rem(t1 + 2, 4)]

    def at_x(d):
        return (me - x + xs[d], t)

    def at_y(d):
        return (me + 4 * (yz[d] - y), t)

    def at_z(d):
        return (me + 16 * (zs[d] - z), t)

    def at_a(d):
        return (me + h * (xs[d] - x) + (1 - h) * 4 * (yz[d] - y), t)

    def at_b(d):
        return (me + (1 - h) * (xs[d] - x) + h * 4 * (yz[d] - y), t)

    def at_t(j):
        return (me, tt[j])

    partners = [f(d) for f in (at_x, at_y, at_z, at_t) for d in range(1, N)]
    barrier = pltpu.get_barrier_semaphore()
    for p in partners:
        pl.semaphore_signal(barrier, inc=1, device_id=p, device_id_type=MESH)

    n_sem = [0]
    sent = []

    def send(src, dst, to):
        i = n_sem[0]
        n_sem[0] += 1
        c = pltpu.make_async_remote_copy(
            src_ref=src,
            dst_ref=dst,
            send_sem=ss.at[i],
            recv_sem=rs.at[i],
            device_id=to,
            device_id_type=MESH,
        )
        c.start()
        sent.append(c)
        return c

    stripe = 16 * b + 4 * a + z
    own_keep = pltpu.make_async_copy(keep_in, keep, ls.at[2])
    own_keep.start()
    own_block = pltpu.make_async_copy(w.at[pl.ds(32 * t, 32)], wx.at[t], ls.at[0])
    own_block.start()
    own_rows = pltpu.make_async_copy(
        w.at[:, pl.ds(pl.multiple_of(16 * (stripe // 16), 16), 16)], wt, ls.at[3]
    )
    own_rows.start()

    gbuf[0, t] = dv[...]
    pl.semaphore_wait(barrier, len(partners))

    g1 = send(gbuf.at[0, t], gbuf.at[0, t], at_t(2))
    g2a = [send(gbuf.at[0, t], gbuf.at[d, t], at_b(d)) for d in range(1, N)]
    g3 = [send(gbuf.at[0, t], gbuf.at[0, t], at_t(1))]
    acts_x, acts_y = [], []
    for d in range(1, N):
        acts_x.append(send(acts.at[:, pl.ds(TILE * xs[d], TILE)], ax.at[0, d - 1], at_x(d)))
        acts_y.append(send(acts.at[:, pl.ds(TILE * yz[d], TILE)], ax.at[1, d - 1], at_y(d)))
    w1core = send(w.at[pl.ds(32 * t1, 32)], wx.at[t], at_t(1))
    at[0, :, :TOK] = acts[:, pl.ds(TILE * x, TILE)].T
    at[1, :, :TOK] = acts[:, pl.ds(TILE * y, TILE)].T
    g1.wait_recv()
    g2b = [send(gbuf.at[0, tt[2]], gbuf.at[d, tt[2]], at_a(d)) for d in range(1, N)]
    g3.append(send(gbuf.at[0, tt[2]], gbuf.at[0, tt[2]], at_t(1)))

    share_x, share_y = 4 * y + x, 16 + 4 * x + y
    w1 = [
        send(w.at[32 * tt[j] + share], wx.at[t, share], at_t(j))
        for j in (2, 3)
        for share in (share_x, share_y)
    ]

    def cut(buf, half, axis, index):
        if axis == "b":
            return buf.at[half, index]
        if axis == "a":
            return buf.at[half, :, index]
        return buf.at[half, :, :, index]

    def hop(buf, stage, half, axis):
        to = {"a": at_a, "b": at_b, "z": at_z}[axis]
        place = {"a": as_, "b": bs, "z": zs}[axis]
        source, target = buf.at[stage], buf.at[stage + 1]
        mine = place[0]
        out = [
            send(cut(source, half, axis, place[d]), cut(target, half, axis, mine), to(d))
            for d in range(1, N)
        ]
        if axis == "b":
            buf[stage + 1, half, mine] = buf[stage, half, mine]
        elif axis == "a":
            buf[stage + 1, half, :, mine] = buf[stage, half, :, mine]
        else:
            buf[stage + 1, half, :, :, mine] = buf[stage, half, :, :, mine]
        return out

    mb[0] = jnp.zeros((2, N, N, N, 4, LANES), F32)
    for q in range(3):
        for half in range(2):
            part = slice(LANES * half, LANES * (half + 1))
            if q < 2:
                chunk = mom[64 * q : 64 * (q + 1), part]
            else:
                chunk = jnp.concatenate([mom[128:CAP, part], jnp.zeros((32, LANES), F32)])
            eb[q, half, :64] = chunk
            eb[q, half, 64:] = chunk
            for i in range(64):
                mb[0, half, i // 16, (i // 4) % 4, i % 4, q : q + 1, :] = eb[
                    q, half, pl.ds(turn_ref[1] + i, 1), :
                ]
    m1 = hop(mb, 0, 0, "z") + hop(mb, 0, 1, "z")
    for d in range(1, N):
        g2a[d - 1].wait_recv()
        g3.append(send(gbuf.at[d, t], gbuf.at[d, t], at_t(1)))
    for d in range(1, N):
        acts_x[d - 1].wait_recv()
        at[0, :, TOK * d : TOK * (d + 1)] = ax[0, d - 1].T
        acts_y[d - 1].wait_recv()
        at[1, :, TOK * d : TOK * (d + 1)] = ax[1, d - 1].T
    for d in range(1, N):
        g2b[d - 1].wait_recv()
        g3.append(send(gbuf.at[d, tt[2]], gbuf.at[d, tt[2]], at_t(1)))
    for c in w1:
        c.wait_recv()
    w2 = []
    for d in range(1, N):
        for j in (2, 3):
            here = wx.at[tt[j], share_x]
            w2.append(send(here, here, at_x(d)))
            here = wx.at[tt[j], share_y]
            w2.append(send(here, here, at_y(d)))
    for c in m1:
        c.wait_recv()
    m2 = hop(mb, 1, 0, "b") + hop(mb, 1, 1, "a")
    for c in g3:
        c.wait_recv()

    first_sums = [None] * N
    order = (0, 2, 1, 3)
    for c in order:
        tile = jnp.dot(
            at[c // 2], gbuf[:, c].reshape(N * TOK, FEAT), preferred_element_type=F32
        )
        for half in range(2):
            part = slice(LANES * half, LANES * (half + 1))
            tb[half] = tile[:, part]
            for s in range(64):
                sb[c, (s // 4) % 4, s % 4, s // 16, :, part] = tb[
                    half, pl.ds(s, 8, stride=64), :
                ]
        to, place = (at_y, yz) if c < 2 else (at_x, xs)
        first_sums[c] = [
            send(sb.at[c, place[d]], yr.at[c, d - 1], to(d)) for d in range(1, N)
        ]
    zcopies = [None] * N
    for c in order:
        for copy in first_sums[c]:
            copy.wait_recv()
        ys[c] = (sb[c, y if c < 2 else x] + yr[c, 0]) + (yr[c, 1] + yr[c, 2])
        zcopies[c] = [send(ys.at[c, zs[d]], zr.at[c, d - 1], at_z(d)) for d in range(1, N)]
    for c in w2:
        c.wait_recv()
    w3 = []
    for c in m2:
        c.wait_recv()
    m3 = hop(mb, 2, 0, "a") + hop(mb, 2, 1, "b")
    quarter_y, quarter_x = pl.ds(4 * y, 4), pl.ds(16 + 4 * x, 4)
    for d in range(1, N):
        for j in (2, 3):
            w3.append(send(wx.at[tt[j], quarter_y], wx.at[tt[j], quarter_y], at_y(d)))
            w3.append(send(wx.at[tt[j], quarter_x], wx.at[tt[j], quarter_x], at_x(d)))
    own_rows.wait()
    lane = lax.broadcasted_iota(jnp.int32, (16, 16, FEAT), 1)

    @pl.loop(0, 8)
    def _(i):
        here = pl.ds(pl.multiple_of(16 * i, 16), 16)
        old[here] = jnp.sum(
            jnp.where(lane == lax.rem(stripe, 16), wt[here].astype(F32), 0.0), axis=1
        )

    for c in order:
        for copy in zcopies[c]:
            copy.wait_recv()
        ts[c] = (ys[c, z] + zr[c, 0]) + (zr[c, 1] + zr[c, 2])

    tcopies = [send(ts.at[tt[j]], tr.at[t], at_t(j)) for j in range(1, N)]
    tr[t] = ts[t]
    for c in m3:
        c.wait_recv()
    for half in range(2):
        for i in range(64):
            flat[half, 4 * i : 4 * i + 4, :] = mb[3, half, i // 16, (i // 4) % 4, i % 4]
        for i in range(HELD):
            held[half, i : i + 1, :] = flat[half, pl.ds(source_ref[i], 1), :]
    for c in tcopies:
        c.wait_recv()
    xcopies = [send(tr.at[:, bs[d]], rr.at[:, b], at_b(d)) for d in range(1, N)]
    rr[:, b] = tr[:, b]
    r2[:, 128:, :] = jnp.zeros((2, 8, LANES), F32)
    for c in xcopies:
        c.wait_recv()
    for i in range(N):
        for j in range(N):
            for half in range(2):
                part = slice(LANES * half, LANES * (half + 1))
                r2[half, 32 * i + 8 * j : 32 * i + 8 * j + 8, :] = rr[i, j, :, part]

    for half in range(2):
        part = slice(LANES * half, LANES * (half + 1))
        moved = momentum_beta * held[half] + (1.0 - momentum_beta) * (
            r2[half, :HELD, :] / total_ref[0]
        )
        r2[half, :HELD, :] = moved
        soft_sign = moved / jnp.sqrt(moved * moved + soft_eps * soft_eps)
        slots[:, part] = (old[:, part] - learn_rate * soft_sign).astype(BF)

    own_slot = pltpu.make_async_copy(slots, es.at[z, y, x], ls.at[1])
    own_slot.start()
    ez = [send(slots, es.at[z, y, x], at_z(d)) for d in range(1, N)]
    for i in range(N):
        for j in range(N):
            for k in range(N):
                first = first_ref[16 * k + (4 - 3 * h) * j + (1 + 3 * h) * i]
                for half in range(2):
                    pb[0, half, i, j, k] = r2[half, pl.ds(first, 4), :]
    p1 = hop(pb, 0, 0, "b") + hop(pb, 0, 1, "a")

    own_block.wait()
    w1core.wait_recv()
    for c in w3:
        c.wait_recv()
    for n in range(N):
        part = pl.ds(512 * n, 512)
        total = jnp.zeros((TOK, 512), F32)
        for c in range(N):
            total = total + lax.dot_general(
                gbuf[0, c],
                wx[c, 8 * n : 8 * n + 8].reshape(512, FEAT),
                (((1,), (1,)), ((), ())),
                preferred_element_type=F32,
            )
        grads_out[:, part] = total.astype(BF)

    own_slot.wait()
    for c in ez:
        c.wait_recv()
    low, high = pl.ds(0, HALF), pl.ds(HALF, HALF)
    near, far = pl.ds(0, 2), pl.ds(2, 2)

    def column(axis, d, zz):
        if axis == "y":
            return es.at[zz, y, lax.rem(x - d + 4, 4), low]
        return es.at[zz, lax.rem(y - d + 4, 4), x, high]

    def passed(axis, d, back, zz):
        if axis == "y":
            return es.at[zz, lax.rem(y - back + 4, 4), lax.rem(x - d + 4, 4), low]
        return es.at[zz, lax.rem(y - d + 4, 4), lax.rem(x - back + 4, 4), high]

    def spread(axis, d):
        to = at_y if axis == "y" else at_x
        out = {}
        for key, zz, step in (("up", near, 1), ("down", far, 3)):
            out[key] = send(column(axis, d, zz), column(axis, d, zz), to(step))
        for key, zz, step in (("up2", far, 1), ("down2", near, 3)):
            out[key] = send(column(axis, d, zz), column(axis, d, zz), to(step))
        return out

    def forward(axis, d, out):
        to = at_y if axis == "y" else at_x
        out["up"].wait_recv()
        here = passed(axis, d, 1, near)
        out["fup"] = send(here, here, to(1))
        out["down"].wait_recv()
        here = passed(axis, d, 3, far)
        out["fdown"] = send(here, here, to(3))

    steps = {
        axis: [
            send(own, own, to(d))
            for to in ((at_x if axis == "y" else at_y),)
            for own in (column(axis, 0, pl.ds(0, 4)),)
            for d in (1, 3, 2)
        ]
        for axis in ("y", "x")
    }
    outs = {axis: [(0, spread(axis, 0))] for axis in ("y", "x")}
    for c in p1:
        c.wait_recv()
    p2 = hop(pb, 1, 0, "a") + hop(pb, 1, 1, "b")
    for i, d in enumerate((1, 3)):
        for axis in ("y", "x"):
            steps[axis][i].wait_recv()
            outs[axis].append((d, spread(axis, d)))
    for axis in ("y", "x"):
        forward(axis, *outs[axis][0])
    for axis in ("y", "x"):
        steps[axis][2].wait_recv()
        outs[axis].append((2, spread(axis, 2)))
    for c in p2:
        c.wait_recv()
    p3 = hop(pb, 2, 0, "z") + hop(pb, 2, 1, "z")
    for i in (1, 2, 3):
        for axis in ("y", "x"):
            forward(axis, *outs[axis][i])
    for c in p3:
        c.wait_recv()
    own_keep.wait()
    for half in range(2):
        part = slice(LANES * half, LANES * (half + 1))
        got = pb[3, half].reshape(REPLICAS, 4, LANES)
        for q in range(3):
            eb[q, half, :64] = got[:, q]
            eb[q, half, 64:] = got[:, q]
        rows = jnp.concatenate(
            [eb[q, half, pl.ds(turn_ref[0], 64), :] for q in range(3)], axis=0
        )[:CAP]
        new_mom[:, part] = keep[...] * rows + (1.0 - keep[...]) * (
            momentum_beta * mom[:, part]
        )
    for axis in ("y", "x"):
        for _, out in outs[axis]:
            for key in ("up2", "down2", "fup", "fdown"):
                out[key].wait_recv()
    for c in sent:
        c.wait_send()


N_COPIES = 173


def prepare_kernel(
    rows_ref,
    owner_ref,
    count_ref,
    dv,
    first_ref,
    source_ref,
    turn_ref,
    total_ref,
    masked,
    keep,
):
    me = lax.axis_index("dp")
    h = lax.axis_index("tensor") // 2
    cx, cy = 16 - 12 * h, 4 + 12 * h
    stripe = cx * lax.rem(me, 4) + cy * lax.rem(me // 4, 4) + me // 16

    def step(p, carry):
        start, mine, length, total = carry
        rows, owner = rows_ref[p], owner_ref[p]
        first = lax.div(start - stripe + 63, 64)
        first_ref[owner] = first
        at = cx * lax.rem(owner, 4) + cy * lax.rem(lax.div(owner, 4), 4) + lax.div(owner, 16)
        for q in range(3):
            source_ref[first + q] = 4 * at + q
        here = owner == me
        return (
            start + rows,
            jnp.where(here, start, mine),
            jnp.where(here, rows, length),
            total + count_ref[p],
        )

    zero = jnp.int32(0)
    _, start, length, total = lax.fori_loop(0, REPLICAS, step, (zero, zero, zero, zero))
    turn_ref[0] = lax.rem(start, 64)
    turn_ref[1] = 64 - lax.rem(start, 64)
    total_ref[0] = total.astype(F32)
    tokens = lax.broadcasted_iota(jnp.int32, (TOK, FEAT), 0)
    masked[...] = jnp.where(tokens < count_ref[me], dv[...], jnp.zeros((TOK, FEAT), BF))
    rows = lax.broadcasted_iota(jnp.int32, (CAP, LANES), 0)
    keep[...] = jnp.where(rows < length, 1.0, 0.0)


def place_kernel(es, out, rows):
    h = lax.axis_index("tensor") // 2
    for s in range(64):
        held = es[16 * (s % 4) + (4 - 3 * h) * ((s // 4) % 4) + (1 + 3 * h) * (s // 16)]
        for half in range(2):
            part = slice(LANES * half, LANES * (half + 1))
            rows[half, pl.ds(s, HELD, stride=64), :] = held[:, part].astype(F32)

    @pl.loop(0, 32)
    def _(i):
        here = pl.ds(pl.multiple_of(i * 256, 256), 256)
        for half in range(2):
            part = slice(LANES * half, LANES * (half + 1))
            out[here, part] = rows[half, here, :].astype(BF)


def local(acts, dv, w, mom, piece_rows, piece_owner, token_counts):
    smem = pl.BlockSpec(memory_space=pltpu.SMEM)
    vmem = pl.BlockSpec(memory_space=pltpu.VMEM)
    hbm = pl.BlockSpec(memory_space=pl.ANY)
    first, source, turn, total, masked, keep = pl.pallas_call(
        prepare_kernel,
        out_shape=(
            jax.ShapeDtypeStruct((REPLICAS,), jnp.int32),
            jax.ShapeDtypeStruct((HELD + 8,), jnp.int32),
            jax.ShapeDtypeStruct((2,), jnp.int32),
            jax.ShapeDtypeStruct((1,), F32),
            jax.ShapeDtypeStruct((TOK, FEAT), BF),
            jax.ShapeDtypeStruct((CAP, LANES), F32),
        ),
        in_specs=[smem, smem, smem, vmem],
        out_specs=(smem, smem, smem, smem, vmem, vmem),
    )(piece_rows, piece_owner, token_counts, dv)
    es, new_mom, input_grads = pl.pallas_call(
        exchange_kernel,
        out_shape=(
            jax.ShapeDtypeStruct((N, N, N, HELD, FEAT), BF),
            jax.ShapeDtypeStruct((CAP, FEAT), F32),
            jax.ShapeDtypeStruct((TOK, BLOCK), BF),
        ),
        in_specs=[smem] * 4 + [vmem, vmem, vmem] + [hbm] * 2,
        out_specs=(vmem, vmem, vmem),
        scratch_shapes=[
            pltpu.VMEM((N, N, TOK, FEAT), BF),
            pltpu.VMEM((2, N - 1, TOK, TILE), BF),
            pltpu.VMEM((2, TILE, N * TOK), BF),
            pltpu.VMEM((N, 32, 64, FEAT), BF),
            pltpu.VMEM((2, TILE, LANES), F32),
            pltpu.VMEM((N, N, N, N, 8, FEAT), F32),
            pltpu.VMEM((N, N - 1, N, N, 8, FEAT), F32),
            pltpu.VMEM((N, N, N, 8, FEAT), F32),
            pltpu.VMEM((N, N - 1, N, 8, FEAT), F32),
            pltpu.VMEM((N, N, 8, FEAT), F32),
            pltpu.VMEM((N, N, 8, FEAT), F32),
            pltpu.VMEM((N, N, 8, FEAT), F32),
            pltpu.VMEM((2, HELD + 8, LANES), F32),
            pltpu.VMEM((4, 2, N, N, N, 4, LANES), F32),
            pltpu.VMEM((4, 2, N, N, N, 4, LANES), F32),
            pltpu.VMEM((2, 256, LANES), F32),
            pltpu.VMEM((2, HELD, LANES), F32),
            pltpu.VMEM((3, 2, 128, LANES), F32),
            pltpu.VMEM((HELD, 16, FEAT), BF),
            pltpu.VMEM((HELD, FEAT), F32),
            pltpu.VMEM((HELD, FEAT), BF),
            pltpu.VMEM((CAP, LANES), F32),
            pltpu.SemaphoreType.DMA((N_COPIES,)),
            pltpu.SemaphoreType.DMA((N_COPIES,)),
            pltpu.SemaphoreType.DMA((4,)),
        ],
        compiler_params=pltpu.CompilerParams(
            collective_id=0, has_side_effects=True, vmem_limit_bytes=32 * 2**20
        ),
    )(
        first,
        source,
        turn,
        total,
        acts,
        masked,
        mom,
        w.reshape(ROWS // 64, 64, FEAT),
        keep,
    )
    new_weight = pl.pallas_call(
        place_kernel,
        out_shape=jax.ShapeDtypeStruct((ROWS, FEAT), BF),
        in_specs=[vmem],
        out_specs=vmem,
        scratch_shapes=[pltpu.VMEM((2, ROWS, LANES), F32)],
        compiler_params=pltpu.CompilerParams(vmem_limit_bytes=24 * 2**20),
    )(es.reshape(REPLICAS, HELD, FEAT))
    return input_grads, new_weight, new_mom


def solution(mesh):
    return jax.shard_map(
        local,
        mesh=mesh,
        in_specs=(
            P("dp", "tensor"),
            P("dp", "tensor"),
            P(None, "tensor"),
            P("dp", "tensor"),
            P(),
            P(),
            P(),
        ),
        out_specs=(P("dp", "tensor"), P(None, "tensor"), P("dp", "tensor")),
        check_vma=False,
    )
```

```python
import jax
import jax.numpy as jnp
from jax import lax
from jax.experimental import pallas as pl
from jax.experimental.pallas import tpu as pltpu
from jax.sharding import PartitionSpec as P

momentum_beta = 0.9
learn_rate = 0.004
soft_eps = 0.0005

N = 4
REPLICAS = 64
CAP = 160
HELD = 128
HALF = 64
TOK = 256
FEAT = 256
LANES = 128
BLOCK = 2048
TILE = 512
ROWS = 8192
MESH = pl.DeviceIdType.MESH
BF = jnp.bfloat16
F32 = jnp.float32


def exchange_kernel(
    table_ref,
    acts,
    packed,
    mom_in,
    w,
    es,
    new_mom,
    grads_out,
    gbuf,
    ax,
    at,
    wx,
    sb,
    yr,
    ys,
    zr,
    ts,
    tr,
    rr,
    r2,
    mb,
    pb,
    flat,
    held,
    eb,
    wt,
    old,
    slots,
    keep,
    mom,
    own,
    ss,
    rs,
    ls,
):
    me = lax.axis_index("dp")
    t = lax.axis_index("tensor")
    x = lax.rem(me, 4)
    y = lax.rem(me // 4, 4)
    z = me // 16
    xs = [lax.rem(x + d, 4) for d in range(N)]
    yz = [lax.rem(y + d, 4) for d in range(N)]
    zs = [lax.rem(z + d, 4) for d in range(N)]
    h = t // 2
    a = h * x + (1 - h) * y
    b = (1 - h) * x + h * y
    as_ = [lax.rem(a + d, 4) for d in range(N)]
    bs = [lax.rem(b + d, 4) for d in range(N)]
    t1 = t + 1 - 2 * lax.rem(t, 2)
    tt = [t, t1, lax.rem(t + 2, 4), lax.rem(t1 + 2, 4)]

    def at_x(d):
        return (me - x + xs[d], t)

    def at_y(d):
        return (me + 4 * (yz[d] - y), t)

    def at_z(d):
        return (me + 16 * (zs[d] - z), t)

    def at_a(d):
        return (me + h * (xs[d] - x) + (1 - h) * 4 * (yz[d] - y), t)

    def at_b(d):
        return (me + (1 - h) * (xs[d] - x) + h * 4 * (yz[d] - y), t)

    def at_t(j):
        return (me, tt[j])

    partners = [f(d) for f in (at_x, at_y, at_z, at_t) for d in range(1, N)]
    barrier = pltpu.get_barrier_semaphore()
    for p in partners:
        pl.semaphore_signal(barrier, inc=1, device_id=p, device_id_type=MESH)

    n_sem = [0]
    sent = []

    def send(src, dst, to):
        i = n_sem[0]
        n_sem[0] += 1
        c = pltpu.make_async_remote_copy(
            src_ref=src,
            dst_ref=dst,
            send_sem=ss.at[i],
            recv_sem=rs.at[i],
            device_id=to,
            device_id_type=MESH,
        )
        c.start()
        sent.append(c)
        return c

    stripe = 16 * b + 4 * a + z
    own_dv = pltpu.make_async_copy(packed.at[pl.ds(0, TOK)], gbuf.at[0, t], ls.at[5])
    own_dv.start()
    own_acts = [
        pltpu.make_async_copy(acts.at[:, pl.ds(TILE * p, TILE)], own.at[i], ls.at[6 + i])
        for i, p in enumerate((x, y))
    ]
    for c in own_acts:
        c.start()
    own_mom = pltpu.make_async_copy(mom_in, mom, ls.at[4])
    own_mom.start()
    own_keep = pltpu.make_async_copy(packed.at[pl.ds(TOK, CAP)], keep, ls.at[2])
    own_keep.start()
    own_block = pltpu.make_async_copy(w.at[pl.ds(32 * t, 32)], wx.at[t], ls.at[0])
    own_block.start()
    own_rows = pltpu.make_async_copy(
        w.at[:, pl.ds(pl.multiple_of(16 * (stripe // 16), 16), 16)], wt, ls.at[3]
    )
    own_rows.start()

    own_dv.wait()
    pl.semaphore_wait(barrier, len(partners))

    g1 = send(gbuf.at[0, t], gbuf.at[0, t], at_t(2))
    g2a = [send(gbuf.at[0, t], gbuf.at[d, t], at_b(d)) for d in range(1, N)]
    g3 = [send(gbuf.at[0, t], gbuf.at[0, t], at_t(1))]
    acts_x, acts_y = [], []
    for d in range(1, N):
        acts_x.append(send(acts.at[:, pl.ds(TILE * xs[d], TILE)], ax.at[0, d - 1], at_x(d)))
        acts_y.append(send(acts.at[:, pl.ds(TILE * yz[d], TILE)], ax.at[1, d - 1], at_y(d)))
    w1core = send(w.at[pl.ds(32 * t1, 32)], wx.at[t], at_t(1))
    for i in range(2):
        own_acts[i].wait()
        at[i, :, :TOK] = own[i].T
    g1.wait_recv()
    g2b = [send(gbuf.at[0, tt[2]], gbuf.at[d, tt[2]], at_a(d)) for d in range(1, N)]
    g3.append(send(gbuf.at[0, tt[2]], gbuf.at[0, tt[2]], at_t(1)))

    share_x, share_y = 4 * y + x, 16 + 4 * x + y
    w1 = [
        send(w.at[32 * tt[j] + share], wx.at[t, share], at_t(j))
        for j in (2, 3)
        for share in (share_x, share_y)
    ]

    def cut(buf, half, axis, index):
        if axis == "b":
            return buf.at[half, index]
        if axis == "a":
            return buf.at[half, :, index]
        return buf.at[half, :, :, index]

    def hop(buf, stage, half, axis):
        to = {"a": at_a, "b": at_b, "z": at_z}[axis]
        place = {"a": as_, "b": bs, "z": zs}[axis]
        source, target = buf.at[stage], buf.at[stage + 1]
        mine = place[0]
        out = [
            send(cut(source, half, axis, place[d]), cut(target, half, axis, mine), to(d))
            for d in range(1, N)
        ]
        if axis == "b":
            buf[stage + 1, half, mine] = buf[stage, half, mine]
        elif axis == "a":
            buf[stage + 1, half, :, mine] = buf[stage, half, :, mine]
        else:
            buf[stage + 1, half, :, :, mine] = buf[stage, half, :, :, mine]
        return out

    own_mom.wait()
    mb[0] = jnp.zeros((2, N, N, N, 4, LANES), F32)
    for q in range(3):
        for half in range(2):
            part = slice(LANES * half, LANES * (half + 1))
            if q < 2:
                chunk = mom[64 * q : 64 * (q + 1), part]
            else:
                chunk = jnp.concatenate([mom[128:CAP, part], jnp.zeros((32, LANES), F32)])
            eb[q, half, :64] = chunk
            eb[q, half, 64:] = chunk
            for i in range(64):
                mb[0, half, i // 16, (i // 4) % 4, i % 4, q : q + 1, :] = eb[
                    q, half, pl.ds(table_ref[201] + i, 1), :
                ]
    m1 = hop(mb, 0, 0, "z") + hop(mb, 0, 1, "z")
    for d in range(1, N):
        g2a[d - 1].wait_recv()
        g3.append(send(gbuf.at[d, t], gbuf.at[d, t], at_t(1)))
    for d in range(1, N):
        acts_x[d - 1].wait_recv()
        at[0, :, TOK * d : TOK * (d + 1)] = ax[0, d - 1].T
        acts_y[d - 1].wait_recv()
        at[1, :, TOK * d : TOK * (d + 1)] = ax[1, d - 1].T
    for d in range(1, N):
        g2b[d - 1].wait_recv()
        g3.append(send(gbuf.at[d, tt[2]], gbuf.at[d, tt[2]], at_t(1)))
    for c in w1:
        c.wait_recv()
    w2 = []
    for d in range(1, N):
        for j in (2, 3):
            here = wx.at[tt[j], share_x]
            w2.append(send(here, here, at_x(d)))
            here = wx.at[tt[j], share_y]
            w2.append(send(here, here, at_y(d)))
    for c in m1:
        c.wait_recv()
    m2 = hop(mb, 1, 0, "b") + hop(mb, 1, 1, "a")
    for c in g3:
        c.wait_recv()

    first_sums = [None] * N
    order = (0, 2, 1, 3)
    for c in order:
        tile = jnp.dot(
            at[c // 2], gbuf[:, c].reshape(N * TOK, FEAT), preferred_element_type=F32
        )
        for half in range(2):
            part = slice(LANES * half, LANES * (half + 1))
            turned = jnp.swapaxes(tile[:, part].reshape(8, 64, LANES), 0, 1)
            for s in range(64):
                sb[c, (s // 4) % 4, s % 4, s // 16, :, part] = turned[s]
        to, place = (at_y, yz) if c < 2 else (at_x, xs)
        first_sums[c] = [
            send(sb.at[c, place[d]], yr.at[c, d - 1], to(d)) for d in range(1, N)
        ]
    zcopies = [None] * N
    for c in order:
        for copy in first_sums[c]:
            copy.wait_recv()
        ys[c] = (sb[c, y if c < 2 else x] + yr[c, 0]) + (yr[c, 1] + yr[c, 2])
        zcopies[c] = [send(ys.at[c, zs[d]], zr.at[c, d - 1], at_z(d)) for d in range(1, N)]
    for c in w2:
        c.wait_recv()
    w3 = []
    for c in m2:
        c.wait_recv()
    m3 = hop(mb, 2, 0, "a") + hop(mb, 2, 1, "b")
    quarter_y, quarter_x = pl.ds(4 * y, 4), pl.ds(16 + 4 * x, 4)
    for d in range(1, N):
        for j in (2, 3):
            w3.append(send(wx.at[tt[j], quarter_y], wx.at[tt[j], quarter_y], at_y(d)))
            w3.append(send(wx.at[tt[j], quarter_x], wx.at[tt[j], quarter_x], at_x(d)))
    own_rows.wait()
    lane = lax.broadcasted_iota(jnp.int32, (16, 16, FEAT), 1)

    @pl.loop(0, 8)
    def _(i):
        here = pl.ds(pl.multiple_of(16 * i, 16), 16)
        old[here] = jnp.sum(
            jnp.where(lane == lax.rem(stripe, 16), wt[here].astype(F32), 0.0), axis=1
        )

    for c in order:
        for copy in zcopies[c]:
            copy.wait_recv()
        ts[c] = (ys[c, z] + zr[c, 0]) + (zr[c, 1] + zr[c, 2])

    tcopies = [send(ts.at[tt[j]], tr.at[t], at_t(j)) for j in range(1, N)]
    tr[t] = ts[t]
    for c in m3:
        c.wait_recv()
    for half in range(2):
        for i in range(64):
            flat[half, 4 * i : 4 * i + 4, :] = mb[3, half, i // 16, (i // 4) % 4, i % 4]
        for i in range(HELD):
            held[half, i : i + 1, :] = flat[half, pl.ds(table_ref[64 + i], 1), :]
    for c in tcopies:
        c.wait_recv()
    xcopies = [send(tr.at[:, bs[d]], rr.at[:, b], at_b(d)) for d in range(1, N)]
    rr[:, b] = tr[:, b]
    r2[:, 128:, :] = jnp.zeros((2, 8, LANES), F32)
    for c in xcopies:
        c.wait_recv()
    for i in range(N):
        for j in range(N):
            for half in range(2):
                part = slice(LANES * half, LANES * (half + 1))
                r2[half, 32 * i + 8 * j : 32 * i + 8 * j + 8, :] = rr[i, j, :, part]

    total = table_ref[202].astype(F32)
    for half in range(2):
        part = slice(LANES * half, LANES * (half + 1))
        moved = momentum_beta * held[half] + (1.0 - momentum_beta) * (
            r2[half, :HELD, :] / total
        )
        r2[half, :HELD, :] = moved
        soft_sign = moved / jnp.sqrt(moved * moved + soft_eps * soft_eps)
        slots[:, part] = (old[:, part] - learn_rate * soft_sign).astype(BF)

    own_slot = pltpu.make_async_copy(slots, es.at[z, y, x], ls.at[1])
    own_slot.start()
    ez = [send(slots, es.at[z, y, x], at_z(d)) for d in range(1, N)]
    for i in range(N):
        for j in range(N):
            for k in range(N):
                first = table_ref[16 * k + (4 - 3 * h) * j + (1 + 3 * h) * i]
                for half in range(2):
                    pb[0, half, i, j, k] = r2[half, pl.ds(first, 4), :]
    p1 = hop(pb, 0, 0, "b") + hop(pb, 0, 1, "a")

    own_block.wait()
    w1core.wait_recv()
    for c in w3:
        c.wait_recv()
    for n in range(N):
        part = pl.ds(512 * n, 512)
        total = jnp.zeros((TOK, 512), F32)
        for c in range(N):
            total = total + lax.dot_general(
                gbuf[0, c],
                wx[c, 8 * n : 8 * n + 8].reshape(512, FEAT),
                (((1,), (1,)), ((), ())),
                preferred_element_type=F32,
            )
        grads_out[:, part] = total.astype(BF)

    own_slot.wait()
    for c in ez:
        c.wait_recv()
    low, high = pl.ds(0, HALF), pl.ds(HALF, HALF)
    near, far = pl.ds(0, 2), pl.ds(2, 2)

    def column(axis, d, zz):
        if axis == "y":
            return es.at[zz, y, lax.rem(x - d + 4, 4), low]
        return es.at[zz, lax.rem(y - d + 4, 4), x, high]

    def passed(axis, d, back, zz):
        if axis == "y":
            return es.at[zz, lax.rem(y - back + 4, 4), lax.rem(x - d + 4, 4), low]
        return es.at[zz, lax.rem(y - d + 4, 4), lax.rem(x - back + 4, 4), high]

    def spread(axis, d):
        to = at_y if axis == "y" else at_x
        out = {}
        for key, zz, step in (("up", near, 1), ("down", far, 3)):
            out[key] = send(column(axis, d, zz), column(axis, d, zz), to(step))
        for key, zz, step in (("up2", far, 1), ("down2", near, 3)):
            out[key] = send(column(axis, d, zz), column(axis, d, zz), to(step))
        return out

    def forward(axis, d, out):
        to = at_y if axis == "y" else at_x
        out["up"].wait_recv()
        here = passed(axis, d, 1, near)
        out["fup"] = send(here, here, to(1))
        out["down"].wait_recv()
        here = passed(axis, d, 3, far)
        out["fdown"] = send(here, here, to(3))

    steps = {
        axis: [
            send(own, own, to(d))
            for to in ((at_x if axis == "y" else at_y),)
            for own in (column(axis, 0, pl.ds(0, 4)),)
            for d in (1, 3, 2)
        ]
        for axis in ("y", "x")
    }
    outs = {axis: [(0, spread(axis, 0))] for axis in ("y", "x")}
    for c in p1:
        c.wait_recv()
    p2 = hop(pb, 1, 0, "a") + hop(pb, 1, 1, "b")
    for i, d in enumerate((1, 3)):
        for axis in ("y", "x"):
            steps[axis][i].wait_recv()
            outs[axis].append((d, spread(axis, d)))
    for axis in ("y", "x"):
        forward(axis, *outs[axis][0])
    for axis in ("y", "x"):
        steps[axis][2].wait_recv()
        outs[axis].append((2, spread(axis, 2)))
    for c in p2:
        c.wait_recv()
    p3 = hop(pb, 2, 0, "z") + hop(pb, 2, 1, "z")
    for i in (1, 2, 3):
        for axis in ("y", "x"):
            forward(axis, *outs[axis][i])
    for c in p3:
        c.wait_recv()
    own_keep.wait()
    for half in range(2):
        part = slice(LANES * half, LANES * (half + 1))
        got = pb[3, half].reshape(REPLICAS, 4, LANES)
        for q in range(3):
            eb[q, half, :64] = got[:, q]
            eb[q, half, 64:] = got[:, q]
        rows = jnp.concatenate(
            [eb[q, half, pl.ds(table_ref[200], 64), :] for q in range(3)], axis=0
        )[:CAP]
        kept = keep[:, :LANES].astype(F32)
        new_mom[:, part] = kept * rows + (1.0 - kept) * (
            momentum_beta * mom[:, part]
        )
    for axis in ("y", "x"):
        for _, out in outs[axis]:
            for key in ("up2", "down2", "fup", "fdown"):
                out[key].wait_recv()
    for c in sent:
        c.wait_send()


N_COPIES = 173


def prepare_kernel(
    rows_ref,
    owner_ref,
    count_ref,
    dv,
    table_ref,
    packed,
):
    me = lax.axis_index("dp")
    h = lax.axis_index("tensor") // 2
    cx, cy = 16 - 12 * h, 4 + 12 * h
    stripe = cx * lax.rem(me, 4) + cy * lax.rem(me // 4, 4) + me // 16

    def step(p, carry):
        start, mine, length, total = carry
        rows, owner = rows_ref[p], owner_ref[p]
        first = lax.div(start - stripe + 63, 64)
        table_ref[owner] = first
        at = cx * lax.rem(owner, 4) + cy * lax.rem(lax.div(owner, 4), 4) + lax.div(owner, 16)
        for q in range(3):
            table_ref[64 + first + q] = 4 * at + q
        here = owner == me
        return (
            start + rows,
            jnp.where(here, start, mine),
            jnp.where(here, rows, length),
            total + count_ref[p],
        )

    zero = jnp.int32(0)
    _, start, length, total = lax.fori_loop(0, REPLICAS, step, (zero, zero, zero, zero))
    table_ref[200] = lax.rem(start, 64)
    table_ref[201] = 64 - lax.rem(start, 64)
    table_ref[202] = total
    tokens = lax.broadcasted_iota(jnp.int32, (TOK, FEAT), 0)
    packed[:TOK, :] = jnp.where(tokens < count_ref[me], dv[...], jnp.zeros((TOK, FEAT), BF))
    rows = lax.broadcasted_iota(jnp.int32, (CAP, FEAT), 0)
    packed[TOK:, :] = jnp.where(rows < length, 1.0, 0.0).astype(BF)


def place_kernel(es, out):
    h = lax.axis_index("tensor") // 2
    for c in range(4):
        for half in range(2):
            part = slice(LANES * half, LANES * (half + 1))
            held = [
                es[16 * (i % 4) + (4 - 3 * h) * (i // 4) + (1 + 3 * h) * c, :, part]
                for i in range(16)
            ]
            rows = jnp.stack([v.astype(F32) for v in held])
            out[:, 16 * c : 16 * (c + 1), part] = jnp.swapaxes(rows, 0, 1).astype(BF)


def local(acts, dv, w, mom, piece_rows, piece_owner, token_counts):
    smem = pl.BlockSpec(memory_space=pltpu.SMEM)
    vmem = pl.BlockSpec(memory_space=pltpu.VMEM)
    hbm = pl.BlockSpec(memory_space=pl.ANY)
    table, packed = pl.pallas_call(
        prepare_kernel,
        out_shape=(
            jax.ShapeDtypeStruct((208,), jnp.int32),
            jax.ShapeDtypeStruct((TOK + CAP, FEAT), BF),
        ),
        in_specs=[smem, smem, smem, vmem],
        out_specs=(smem, vmem),
    )(piece_rows, piece_owner, token_counts, dv)
    es, new_mom, input_grads = pl.pallas_call(
        exchange_kernel,
        out_shape=(
            jax.ShapeDtypeStruct((N, N, N, HELD, FEAT), BF),
            jax.ShapeDtypeStruct((CAP, FEAT), F32),
            jax.ShapeDtypeStruct((TOK, BLOCK), BF),
        ),
        in_specs=[smem] + [hbm] * 4,
        out_specs=(hbm, vmem, vmem),
        scratch_shapes=[
            pltpu.VMEM((N, N, TOK, FEAT), BF),
            pltpu.VMEM((2, N - 1, TOK, TILE), BF),
            pltpu.VMEM((2, TILE, N * TOK), BF),
            pltpu.VMEM((N, 32, 64, FEAT), BF),
            pltpu.VMEM((N, N, N, N, 8, FEAT), F32),
            pltpu.VMEM((N, N - 1, N, N, 8, FEAT), F32),
            pltpu.VMEM((N, N, N, 8, FEAT), F32),
            pltpu.VMEM((N, N - 1, N, 8, FEAT), F32),
            pltpu.VMEM((N, N, 8, FEAT), F32),
            pltpu.VMEM((N, N, 8, FEAT), F32),
            pltpu.VMEM((N, N, 8, FEAT), F32),
            pltpu.VMEM((2, HELD + 8, LANES), F32),
            pltpu.VMEM((4, 2, N, N, N, 4, LANES), F32),
            pltpu.VMEM((4, 2, N, N, N, 4, LANES), F32),
            pltpu.VMEM((2, 256, LANES), F32),
            pltpu.VMEM((2, HELD, LANES), F32),
            pltpu.VMEM((3, 2, 128, LANES), F32),
            pltpu.VMEM((HELD, 16, FEAT), BF),
            pltpu.VMEM((HELD, FEAT), F32),
            pltpu.VMEM((HELD, FEAT), BF),
            pltpu.VMEM((CAP, FEAT), BF),
            pltpu.VMEM((CAP, FEAT), F32),
            pltpu.VMEM((2, TOK, TILE), BF),
            pltpu.SemaphoreType.DMA((N_COPIES,)),
            pltpu.SemaphoreType.DMA((N_COPIES,)),
            pltpu.SemaphoreType.DMA((8,)),
        ],
        compiler_params=pltpu.CompilerParams(
            collective_id=0, has_side_effects=True, vmem_limit_bytes=54 * 2**20
        ),
    )(table, acts, packed, mom, w.reshape(ROWS // 64, 64, FEAT))
    new_weight = pl.pallas_call(
        place_kernel,
        out_shape=jax.ShapeDtypeStruct((HELD, 64, FEAT), BF),
        grid=(8,),
        in_specs=[pl.BlockSpec((REPLICAS, 16, FEAT), lambda i: (0, i, 0))],
        out_specs=pl.BlockSpec((16, 64, FEAT), lambda i: (i, 0, 0)),
        compiler_params=pltpu.CompilerParams(vmem_limit_bytes=54 * 2**20),
    )(es.reshape(REPLICAS, HELD, FEAT)).reshape(ROWS, FEAT)
    return input_grads, new_weight, new_mom


def solution(mesh):
    return jax.shard_map(
        local,
        mesh=mesh,
        in_specs=(
            P("dp", "tensor"),
            P("dp", "tensor"),
            P(None, "tensor"),
            P("dp", "tensor"),
            P(),
            P(),
            P(),
        ),
        out_specs=(P("dp", "tensor"), P(None, "tensor"), P("dp", "tensor")),
        check_vma=False,
    )
```

```python
import jax
import jax.numpy as jnp
from jax import lax
from jax.experimental import pallas as pl
from jax.experimental.pallas import tpu as pltpu
from jax.sharding import PartitionSpec as P

momentum_beta = 0.9
learn_rate = 0.004
soft_eps = 0.0005

N = 4
REPLICAS = 64
CAP = 160
HELD = 128
HALF = 64
TOK = 256
FEAT = 256
LANES = 128
BLOCK = 2048
TILE = 512
ROWS = 8192
MESH = pl.DeviceIdType.MESH
BF = jnp.bfloat16
F32 = jnp.float32


def exchange_kernel(
    table_ref,
    acts,
    packed,
    mom_in,
    w,
    es,
    new_mom,
    grads_out,
    gbuf,
    ax,
    at,
    wx,
    sb,
    yr,
    ys,
    zr,
    ts,
    tr,
    rr,
    r2,
    mb,
    pb,
    flat,
    held,
    eb,
    wt,
    old,
    slots,
    keep,
    mom,
    own,
    ss,
    rs,
    ls,
):
    me = lax.axis_index("dp")
    t = lax.axis_index("tensor")
    x = lax.rem(me, 4)
    y = lax.rem(me // 4, 4)
    z = me // 16
    xs = [lax.rem(x + d, 4) for d in range(N)]
    yz = [lax.rem(y + d, 4) for d in range(N)]
    zs = [lax.rem(z + d, 4) for d in range(N)]
    h = t // 2
    a = h * x + (1 - h) * y
    b = (1 - h) * x + h * y
    as_ = [lax.rem(a + d, 4) for d in range(N)]
    bs = [lax.rem(b + d, 4) for d in range(N)]
    t1 = t + 1 - 2 * lax.rem(t, 2)
    tt = [t, t1, lax.rem(t + 2, 4), lax.rem(t1 + 2, 4)]

    def at_x(d):
        return (me - x + xs[d], t)

    def at_y(d):
        return (me + 4 * (yz[d] - y), t)

    def at_z(d):
        return (me + 16 * (zs[d] - z), t)

    def at_a(d):
        return (me + h * (xs[d] - x) + (1 - h) * 4 * (yz[d] - y), t)

    def at_b(d):
        return (me + (1 - h) * (xs[d] - x) + h * 4 * (yz[d] - y), t)

    def at_t(j):
        return (me, tt[j])

    partners = [f(d) for f in (at_x, at_y, at_z, at_t) for d in range(1, N)]
    barrier = pltpu.get_barrier_semaphore()
    for p in partners:
        pl.semaphore_signal(barrier, inc=1, device_id=p, device_id_type=MESH)

    n_sem = [0]
    sent = []

    def send(src, dst, to):
        i = n_sem[0]
        n_sem[0] += 1
        c = pltpu.make_async_remote_copy(
            src_ref=src,
            dst_ref=dst,
            send_sem=ss.at[i],
            recv_sem=rs.at[i],
            device_id=to,
            device_id_type=MESH,
        )
        c.start()
        sent.append(c)
        return c

    stripe = 16 * b + 4 * a + z
    own_dv = pltpu.make_async_copy(packed.at[pl.ds(0, TOK)], gbuf.at[0, t], ls.at[5])
    own_dv.start()
    own_acts = [
        pltpu.make_async_copy(acts.at[:, pl.ds(TILE * p, TILE)], own.at[i], ls.at[6 + i])
        for i, p in enumerate((x, y))
    ]
    for c in own_acts:
        c.start()
    own_mom = pltpu.make_async_copy(mom_in, mom, ls.at[4])
    own_mom.start()
    own_keep = pltpu.make_async_copy(packed.at[pl.ds(TOK, CAP)], keep, ls.at[2])
    own_keep.start()
    own_block = pltpu.make_async_copy(w.at[pl.ds(32 * t, 32)], wx.at[t], ls.at[0])
    own_block.start()
    own_rows = pltpu.make_async_copy(
        w.at[:, pl.ds(pl.multiple_of(16 * (stripe // 16), 16), 16)], wt, ls.at[3]
    )
    own_rows.start()

    own_dv.wait()
    pl.semaphore_wait(barrier, len(partners))

    g1 = send(gbuf.at[0, t], gbuf.at[0, t], at_t(2))
    g2a = [send(gbuf.at[0, t], gbuf.at[d, t], at_b(d)) for d in range(1, N)]
    g3 = [send(gbuf.at[0, t], gbuf.at[0, t], at_t(1))]
    acts_x, acts_y = [], []
    for d in range(1, N):
        acts_x.append(send(acts.at[:, pl.ds(TILE * xs[d], TILE)], ax.at[0, d - 1], at_x(d)))
        acts_y.append(send(acts.at[:, pl.ds(TILE * yz[d], TILE)], ax.at[1, d - 1], at_y(d)))
    w1core = send(w.at[pl.ds(32 * t1, 32)], wx.at[t], at_t(1))
    for i in range(2):
        own_acts[i].wait()
        at[i, :, :TOK] = own[i].T
    g1.wait_recv()
    g2b = [send(gbuf.at[0, tt[2]], gbuf.at[d, tt[2]], at_a(d)) for d in range(1, N)]
    g3.append(send(gbuf.at[0, tt[2]], gbuf.at[0, tt[2]], at_t(1)))

    share_x, share_y = 4 * y + x, 16 + 4 * x + y
    w1 = [
        send(w.at[32 * tt[j] + share], wx.at[t, share], at_t(j))
        for j in (2, 3)
        for share in (share_x, share_y)
    ]

    def cut(buf, half, axis, index):
        if axis == "b":
            return buf.at[half, index]
        if axis == "a":
            return buf.at[half, :, index]
        return buf.at[half, :, :, index]

    def hop(buf, stage, half, axis):
        to = {"a": at_a, "b": at_b, "z": at_z}[axis]
        place = {"a": as_, "b": bs, "z": zs}[axis]
        source, target = buf.at[stage], buf.at[stage + 1]
        mine = place[0]
        out = [
            send(cut(source, half, axis, place[d]), cut(target, half, axis, mine), to(d))
            for d in range(1, N)
        ]
        if axis == "b":
            buf[stage + 1, half, mine] = buf[stage, half, mine]
        elif axis == "a":
            buf[stage + 1, half, :, mine] = buf[stage, half, :, mine]
        else:
            buf[stage + 1, half, :, :, mine] = buf[stage, half, :, :, mine]
        return out

    own_mom.wait()
    mb[0] = jnp.zeros((2, N, N, N, 4, LANES), F32)
    for q in range(3):
        for half in range(2):
            part = slice(LANES * half, LANES * (half + 1))
            if q < 2:
                chunk = mom[64 * q : 64 * (q + 1), part]
            else:
                chunk = jnp.concatenate([mom[128:CAP, part], jnp.zeros((32, LANES), F32)])
            eb[q, half, :64] = chunk
            eb[q, half, 64:] = chunk
            for i in range(64):
                mb[0, half, i // 16, (i // 4) % 4, i % 4, q : q + 1, :] = eb[
                    q, half, pl.ds(table_ref[201] + i, 1), :
                ]
    m1 = hop(mb, 0, 0, "z") + hop(mb, 0, 1, "z")
    for d in range(1, N):
        g2a[d - 1].wait_recv()
        g3.append(send(gbuf.at[d, t], gbuf.at[d, t], at_t(1)))
    for d in range(1, N):
        acts_x[d - 1].wait_recv()
        at[0, :, TOK * d : TOK * (d + 1)] = ax[0, d - 1].T
        acts_y[d - 1].wait_recv()
        at[1, :, TOK * d : TOK * (d + 1)] = ax[1, d - 1].T
    for d in range(1, N):
        g2b[d - 1].wait_recv()
        g3.append(send(gbuf.at[d, tt[2]], gbuf.at[d, tt[2]], at_t(1)))
    for c in w1:
        c.wait_recv()
    w2 = []
    for d in range(1, N):
        for j in (2, 3):
            here = wx.at[tt[j], share_x]
            w2.append(send(here, here, at_x(d)))
            here = wx.at[tt[j], share_y]
            w2.append(send(here, here, at_y(d)))
    for c in m1:
        c.wait_recv()
    m2 = hop(mb, 1, 0, "b") + hop(mb, 1, 1, "a")
    for c in g3:
        c.wait_recv()

    first_sums = [None] * N
    order = (0, 2, 1, 3)
    for c in order:
        tile = jnp.dot(
            at[c // 2], gbuf[:, c].reshape(N * TOK, FEAT), preferred_element_type=F32
        )
        for half in range(2):
            part = slice(LANES * half, LANES * (half + 1))
            turned = jnp.swapaxes(tile[:, part].reshape(8, 64, LANES), 0, 1)
            for s in range(64):
                sb[c, (s // 4) % 4, s % 4, s // 16, :, part] = turned[s]
        to, place = (at_y, yz) if c < 2 else (at_x, xs)
        first_sums[c] = [
            send(sb.at[c, place[d]], yr.at[c, d - 1], to(d)) for d in range(1, N)
        ]
    zcopies = [None] * N
    for c in order:
        for copy in first_sums[c]:
            copy.wait_recv()
        ys[c] = (sb[c, y if c < 2 else x] + yr[c, 0]) + (yr[c, 1] + yr[c, 2])
        zcopies[c] = [send(ys.at[c, zs[d]], zr.at[c, d - 1], at_z(d)) for d in range(1, N)]
    for c in w2:
        c.wait_recv()
    w3 = []
    for c in m2:
        c.wait_recv()
    m3 = hop(mb, 2, 0, "a") + hop(mb, 2, 1, "b")
    quarter_y, quarter_x = pl.ds(4 * y, 4), pl.ds(16 + 4 * x, 4)
    for d in range(1, N):
        for j in (2, 3):
            w3.append(send(wx.at[tt[j], quarter_y], wx.at[tt[j], quarter_y], at_y(d)))
            w3.append(send(wx.at[tt[j], quarter_x], wx.at[tt[j], quarter_x], at_x(d)))
    own_rows.wait()
    lane = lax.broadcasted_iota(jnp.int32, (16, 16, FEAT), 1)

    @pl.loop(0, 8)
    def _(i):
        here = pl.ds(pl.multiple_of(16 * i, 16), 16)
        old[here] = jnp.sum(
            jnp.where(lane == lax.rem(stripe, 16), wt[here].astype(F32), 0.0), axis=1
        )

    for c in order:
        for copy in zcopies[c]:
            copy.wait_recv()
        ts[c] = (ys[c, z] + zr[c, 0]) + (zr[c, 1] + zr[c, 2])

    tcopies = [send(ts.at[tt[j]], tr.at[t], at_t(j)) for j in range(1, N)]
    tr[t] = ts[t]
    for c in m3:
        c.wait_recv()
    for half in range(2):
        for i in range(64):
            flat[half, 4 * i : 4 * i + 4, :] = mb[3, half, i // 16, (i // 4) % 4, i % 4]
        for i in range(HELD):
            held[half, i : i + 1, :] = flat[half, pl.ds(table_ref[64 + i], 1), :]
    for c in tcopies:
        c.wait_recv()
    xcopies = [send(tr.at[:, bs[d]], rr.at[:, b], at_b(d)) for d in range(1, N)]
    rr[:, b] = tr[:, b]
    r2[:, 128:, :] = jnp.zeros((2, 8, LANES), F32)
    for c in xcopies:
        c.wait_recv()
    for i in range(N):
        for j in range(N):
            for half in range(2):
                part = slice(LANES * half, LANES * (half + 1))
                r2[half, 32 * i + 8 * j : 32 * i + 8 * j + 8, :] = rr[i, j, :, part]

    total = table_ref[202].astype(F32)
    for half in range(2):
        part = slice(LANES * half, LANES * (half + 1))
        moved = momentum_beta * held[half] + (1.0 - momentum_beta) * (
            r2[half, :HELD, :] / total
        )
        r2[half, :HELD, :] = moved
        soft_sign = moved / jnp.sqrt(moved * moved + soft_eps * soft_eps)
        slots[:, part] = (old[:, part] - learn_rate * soft_sign).astype(BF)

    own_slot = pltpu.make_async_copy(slots, es.at[z, y, x], ls.at[1])
    own_slot.start()
    ez = [send(slots, es.at[z, y, x], at_z(d)) for d in range(1, N)]
    for i in range(N):
        for j in range(N):
            for k in range(N):
                first = table_ref[16 * k + (4 - 3 * h) * j + (1 + 3 * h) * i]
                for half in range(2):
                    pb[0, half, i, j, k] = r2[half, pl.ds(first, 4), :]
    p1 = hop(pb, 0, 0, "b") + hop(pb, 0, 1, "a")

    own_block.wait()
    w1core.wait_recv()
    for c in w3:
        c.wait_recv()
    for n in range(N):
        part = pl.ds(512 * n, 512)
        total = jnp.zeros((TOK, 512), F32)
        for c in range(N):
            total = total + lax.dot_general(
                gbuf[0, c],
                wx[c, 8 * n : 8 * n + 8].reshape(512, FEAT),
                (((1,), (1,)), ((), ())),
                preferred_element_type=F32,
            )
        grads_out[:, part] = total.astype(BF)

    own_slot.wait()
    for c in ez:
        c.wait_recv()
    low, high = pl.ds(0, HALF), pl.ds(HALF, HALF)
    near, far = pl.ds(0, 2), pl.ds(2, 2)

    def column(axis, d, zz):
        if axis == "y":
            return es.at[zz, y, lax.rem(x - d + 4, 4), low]
        return es.at[zz, lax.rem(y - d + 4, 4), x, high]

    def passed(axis, d, back, zz):
        if axis == "y":
            return es.at[zz, lax.rem(y - back + 4, 4), lax.rem(x - d + 4, 4), low]
        return es.at[zz, lax.rem(y - d + 4, 4), lax.rem(x - back + 4, 4), high]

    def spread(axis, d):
        to = at_y if axis == "y" else at_x
        out = {}
        for key, zz, step in (("up", near, 1), ("down", far, 3)):
            out[key] = send(column(axis, d, zz), column(axis, d, zz), to(step))
        for key, zz, step in (("up2", far, 1), ("down2", near, 3)):
            out[key] = send(column(axis, d, zz), column(axis, d, zz), to(step))
        return out

    def forward(axis, d, out):
        to = at_y if axis == "y" else at_x
        out["up"].wait_recv()
        here = passed(axis, d, 1, near)
        out["fup"] = send(here, here, to(1))
        out["down"].wait_recv()
        here = passed(axis, d, 3, far)
        out["fdown"] = send(here, here, to(3))

    steps = {
        axis: [
            send(own, own, to(d))
            for to in ((at_x if axis == "y" else at_y),)
            for own in (column(axis, 0, pl.ds(0, 4)),)
            for d in (1, 3, 2)
        ]
        for axis in ("y", "x")
    }
    outs = {axis: [(0, spread(axis, 0))] for axis in ("y", "x")}
    for c in p1:
        c.wait_recv()
    p2 = hop(pb, 1, 0, "a") + hop(pb, 1, 1, "b")
    for i, d in enumerate((1, 3)):
        for axis in ("y", "x"):
            steps[axis][i].wait_recv()
            outs[axis].append((d, spread(axis, d)))
    for axis in ("y", "x"):
        forward(axis, *outs[axis][0])
    for axis in ("y", "x"):
        steps[axis][2].wait_recv()
        outs[axis].append((2, spread(axis, 2)))
    for i in (1, 2, 3):
        for axis in ("y", "x"):
            forward(axis, *outs[axis][i])
        if i == 1:
            for c in p2:
                c.wait_recv()
            p3 = hop(pb, 2, 0, "z") + hop(pb, 2, 1, "z")
    for c in p3:
        c.wait_recv()
    own_keep.wait()
    for half in range(2):
        part = slice(LANES * half, LANES * (half + 1))
        got = pb[3, half].reshape(REPLICAS, 4, LANES)
        for q in range(3):
            eb[q, half, :64] = got[:, q]
            eb[q, half, 64:] = got[:, q]
        rows = jnp.concatenate(
            [eb[q, half, pl.ds(table_ref[200], 64), :] for q in range(3)], axis=0
        )[:CAP]
        kept = keep[:, :LANES].astype(F32)
        new_mom[:, part] = kept * rows + (1.0 - kept) * (
            momentum_beta * mom[:, part]
        )
    for axis in ("y", "x"):
        for _, out in outs[axis]:
            for key in ("up2", "down2", "fup", "fdown"):
                out[key].wait_recv()
    for c in sent:
        c.wait_send()


N_COPIES = 173


def prepare_kernel(
    rows_ref,
    owner_ref,
    count_ref,
    dv,
    table_ref,
    packed,
):
    me = lax.axis_index("dp")
    h = lax.axis_index("tensor") // 2
    cx, cy = 16 - 12 * h, 4 + 12 * h
    stripe = cx * lax.rem(me, 4) + cy * lax.rem(me // 4, 4) + me // 16

    def step(p, carry):
        start, mine, length, total = carry
        rows, owner = rows_ref[p], owner_ref[p]
        first = lax.div(start - stripe + 63, 64)
        table_ref[owner] = first
        at = cx * lax.rem(owner, 4) + cy * lax.rem(lax.div(owner, 4), 4) + lax.div(owner, 16)
        for q in range(3):
            table_ref[64 + first + q] = 4 * at + q
        here = owner == me
        return (
            start + rows,
            jnp.where(here, start, mine),
            jnp.where(here, rows, length),
            total + count_ref[p],
        )

    zero = jnp.int32(0)
    _, start, length, total = lax.fori_loop(0, REPLICAS, step, (zero, zero, zero, zero))
    table_ref[200] = lax.rem(start, 64)
    table_ref[201] = 64 - lax.rem(start, 64)
    table_ref[202] = total
    tokens = lax.broadcasted_iota(jnp.int32, (TOK, FEAT), 0)
    packed[:TOK, :] = jnp.where(tokens < count_ref[me], dv[...], jnp.zeros((TOK, FEAT), BF))
    rows = lax.broadcasted_iota(jnp.int32, (CAP, FEAT), 0)
    packed[TOK:, :] = jnp.where(rows < length, 1.0, 0.0).astype(BF)


def place_kernel(es, out, held, rows, in_sem, out_sem):
    h = lax.axis_index("tensor") // 2
    steps = HELD // 16
    fetch = [
        pltpu.make_async_copy(
            es.at[:, pl.ds(16 * n, 16)], held.at[:, pl.ds(16 * n, 16)], in_sem.at[n]
        )
        for n in range(steps)
    ]
    for c in fetch:
        c.start()
    row = lax.broadcasted_iota(jnp.int32, (256, 256), 0)
    column = lax.broadcasted_iota(jnp.int32, (256, 256), 1)
    swap = jnp.where(column == 16 * (row & 15) + (row >> 4), 1.0, 0.0).astype(BF)
    store = []
    for n in range(steps):
        here = pl.ds(16 * n, 16)
        fetch[n].wait()
        for c in range(4):
            slabs = jnp.concatenate(
                [
                    held[16 * (i % 4) + (4 - 3 * h) * (i // 4) + (1 + 3 * h) * c, here]
                    for i in range(16)
                ]
            )
            slabs = jnp.dot(swap, slabs, preferred_element_type=F32).astype(BF)
            rows[here, 16 * c : 16 * (c + 1), :] = slabs.reshape(16, 16, FEAT)
        store.append(pltpu.make_async_copy(rows.at[here], out.at[here], out_sem.at[n]))
        store[-1].start()
    for c in store:
        c.wait()


def local(acts, dv, w, mom, piece_rows, piece_owner, token_counts):
    smem = pl.BlockSpec(memory_space=pltpu.SMEM)
    vmem = pl.BlockSpec(memory_space=pltpu.VMEM)
    hbm = pl.BlockSpec(memory_space=pl.ANY)
    table, packed = pl.pallas_call(
        prepare_kernel,
        out_shape=(
            jax.ShapeDtypeStruct((208,), jnp.int32),
            jax.ShapeDtypeStruct((TOK + CAP, FEAT), BF),
        ),
        in_specs=[smem, smem, smem, vmem],
        out_specs=(smem, vmem),
    )(piece_rows, piece_owner, token_counts, dv)
    es, new_mom, input_grads = pl.pallas_call(
        exchange_kernel,
        out_shape=(
            jax.ShapeDtypeStruct((N, N, N, HELD, FEAT), BF),
            jax.ShapeDtypeStruct((CAP, FEAT), F32),
            jax.ShapeDtypeStruct((TOK, BLOCK), BF),
        ),
        in_specs=[smem] + [hbm] * 4,
        out_specs=(hbm, vmem, vmem),
        scratch_shapes=[
            pltpu.VMEM((N, N, TOK, FEAT), BF),
            pltpu.VMEM((2, N - 1, TOK, TILE), BF),
            pltpu.VMEM((2, TILE, N * TOK), BF),
            pltpu.VMEM((N, 32, 64, FEAT), BF),
            pltpu.VMEM((N, N, N, N, 8, FEAT), F32),
            pltpu.VMEM((N, N - 1, N, N, 8, FEAT), F32),
            pltpu.VMEM((N, N, N, 8, FEAT), F32),
            pltpu.VMEM((N, N - 1, N, 8, FEAT), F32),
            pltpu.VMEM((N, N, 8, FEAT), F32),
            pltpu.VMEM((N, N, 8, FEAT), F32),
            pltpu.VMEM((N, N, 8, FEAT), F32),
            pltpu.VMEM((2, HELD + 8, LANES), F32),
            pltpu.VMEM((4, 2, N, N, N, 4, LANES), F32),
            pltpu.VMEM((4, 2, N, N, N, 4, LANES), F32),
            pltpu.VMEM((2, 256, LANES), F32),
            pltpu.VMEM((2, HELD, LANES), F32),
            pltpu.VMEM((3, 2, 128, LANES), F32),
            pltpu.VMEM((HELD, 16, FEAT), BF),
            pltpu.VMEM((HELD, FEAT), F32),
            pltpu.VMEM((HELD, FEAT), BF),
            pltpu.VMEM((CAP, FEAT), BF),
            pltpu.VMEM((CAP, FEAT), F32),
            pltpu.VMEM((2, TOK, TILE), BF),
            pltpu.SemaphoreType.DMA((N_COPIES,)),
            pltpu.SemaphoreType.DMA((N_COPIES,)),
            pltpu.SemaphoreType.DMA((8,)),
        ],
        compiler_params=pltpu.CompilerParams(
            collective_id=0, has_side_effects=True, vmem_limit_bytes=54 * 2**20
        ),
    )(table, acts, packed, mom, w.reshape(ROWS // 64, 64, FEAT))
    new_weight = pl.pallas_call(
        place_kernel,
        out_shape=jax.ShapeDtypeStruct((HELD, 64, FEAT), BF),
        in_specs=[hbm],
        out_specs=hbm,
        scratch_shapes=[
            pltpu.VMEM((REPLICAS, HELD, FEAT), BF),
            pltpu.VMEM((HELD, 64, FEAT), BF),
            pltpu.SemaphoreType.DMA((HELD // 16,)),
            pltpu.SemaphoreType.DMA((HELD // 16,)),
        ],
        compiler_params=pltpu.CompilerParams(vmem_limit_bytes=54 * 2**20),
    )(es.reshape(REPLICAS, HELD, FEAT)).reshape(ROWS, FEAT)
    return input_grads, new_weight, new_mom


def solution(mesh):
    return jax.shard_map(
        local,
        mesh=mesh,
        in_specs=(
            P("dp", "tensor"),
            P("dp", "tensor"),
            P(None, "tensor"),
            P("dp", "tensor"),
            P(),
            P(),
            P(),
        ),
        out_specs=(P("dp", "tensor"), P(None, "tensor"), P("dp", "tensor")),
        check_vma=False,
    )
```

```python
import jax
import jax.numpy as jnp
from jax import lax
from jax.experimental import pallas as pl
from jax.experimental.pallas import tpu as pltpu
from jax.sharding import PartitionSpec as P

momentum_beta = 0.9
learn_rate = 0.004
soft_eps = 0.0005

N = 4
REPLICAS = 64
CAP = 160
HELD = 128
HALF = 64
TOK = 256
FEAT = 256
LANES = 128
BLOCK = 2048
TILE = 512
ROWS = 8192
MESH = pl.DeviceIdType.MESH
BF = jnp.bfloat16
F32 = jnp.float32


def exchange_kernel(
    table_ref,
    acts,
    packed,
    mom_in,
    w,
    es,
    new_mom,
    grads_hbm,
    gbuf,
    ax,
    at,
    wx,
    sb,
    yr,
    ys,
    zr,
    ts,
    tr,
    rr,
    r2,
    mb,
    pb,
    flat,
    held,
    eb,
    wt,
    old,
    slots,
    keep,
    mom,
    own,
    grads_out,
    ss,
    rs,
    ls,
):
    me = lax.axis_index("dp")
    t = lax.axis_index("tensor")
    x = lax.rem(me, 4)
    y = lax.rem(me // 4, 4)
    z = me // 16
    xs = [lax.rem(x + d, 4) for d in range(N)]
    yz = [lax.rem(y + d, 4) for d in range(N)]
    zs = [lax.rem(z + d, 4) for d in range(N)]
    h = t // 2
    a = h * x + (1 - h) * y
    b = (1 - h) * x + h * y
    as_ = [lax.rem(a + d, 4) for d in range(N)]
    bs = [lax.rem(b + d, 4) for d in range(N)]
    t1 = t + 1 - 2 * lax.rem(t, 2)
    tt = [t, t1, lax.rem(t + 2, 4), lax.rem(t1 + 2, 4)]

    def at_x(d):
        return (me - x + xs[d], t)

    def at_y(d):
        return (me + 4 * (yz[d] - y), t)

    def at_z(d):
        return (me + 16 * (zs[d] - z), t)

    def at_a(d):
        return (me + h * (xs[d] - x) + (1 - h) * 4 * (yz[d] - y), t)

    def at_b(d):
        return (me + (1 - h) * (xs[d] - x) + h * 4 * (yz[d] - y), t)

    def at_t(j):
        return (me, tt[j])

    partners = [f(d) for f in (at_x, at_y, at_z, at_t) for d in range(1, N)]
    barrier = pltpu.get_barrier_semaphore()
    for p in partners:
        pl.semaphore_signal(barrier, inc=1, device_id=p, device_id_type=MESH)

    n_sem = [0]
    sent = []

    def send(src, dst, to):
        i = n_sem[0]
        n_sem[0] += 1
        c = pltpu.make_async_remote_copy(
            src_ref=src,
            dst_ref=dst,
            send_sem=ss.at[i],
            recv_sem=rs.at[i],
            device_id=to,
            device_id_type=MESH,
        )
        c.start()
        sent.append(c)
        return c

    stripe = 16 * b + 4 * a + z
    own_dv = pltpu.make_async_copy(packed.at[pl.ds(0, TOK)], gbuf.at[0, t], ls.at[5])
    own_dv.start()
    own_acts = [
        pltpu.make_async_copy(acts.at[:, pl.ds(TILE * p, TILE)], own.at[i], ls.at[6 + i])
        for i, p in enumerate((x, y))
    ]
    for c in own_acts:
        c.start()
    own_mom = pltpu.make_async_copy(mom_in, mom, ls.at[4])
    own_mom.start()
    own_keep = pltpu.make_async_copy(packed.at[pl.ds(TOK, CAP)], keep, ls.at[2])
    own_keep.start()
    own_block = pltpu.make_async_copy(w.at[pl.ds(32 * t, 32)], wx.at[t], ls.at[0])
    own_block.start()
    own_rows = pltpu.make_async_copy(
        w.at[:, pl.ds(pl.multiple_of(16 * (stripe // 16), 16), 16)], wt, ls.at[3]
    )
    own_rows.start()

    own_dv.wait()
    pl.semaphore_wait(barrier, len(partners))

    g1 = send(gbuf.at[0, t], gbuf.at[0, t], at_t(2))
    g2a = [send(gbuf.at[0, t], gbuf.at[d, t], at_b(d)) for d in range(1, N)]
    g3 = [send(gbuf.at[0, t], gbuf.at[0, t], at_t(1))]
    acts_x, acts_y = [], []
    for d in range(1, N):
        acts_x.append(send(acts.at[:, pl.ds(TILE * xs[d], TILE)], ax.at[0, d - 1], at_x(d)))
        acts_y.append(send(acts.at[:, pl.ds(TILE * yz[d], TILE)], ax.at[1, d - 1], at_y(d)))
    w1core = send(w.at[pl.ds(32 * t1, 32)], wx.at[t], at_t(1))
    for i in range(2):
        own_acts[i].wait()
        at[i, :, :TOK] = own[i].T
    g1.wait_recv()
    g2b = [send(gbuf.at[0, tt[2]], gbuf.at[d, tt[2]], at_a(d)) for d in range(1, N)]
    g3.append(send(gbuf.at[0, tt[2]], gbuf.at[0, tt[2]], at_t(1)))

    share_x, share_y = 4 * y + x, 16 + 4 * x + y
    w1 = [
        send(w.at[32 * tt[j] + share], wx.at[t, share], at_t(j))
        for j in (2, 3)
        for share in (share_x, share_y)
    ]

    def cut(buf, half, axis, index):
        if axis == "b":
            return buf.at[half, index]
        if axis == "a":
            return buf.at[half, :, index]
        return buf.at[half, :, :, index]

    def hop(buf, stage, half, axis):
        to = {"a": at_a, "b": at_b, "z": at_z}[axis]
        place = {"a": as_, "b": bs, "z": zs}[axis]
        source, target = buf.at[stage], buf.at[stage + 1]
        mine = place[0]
        out = [
            send(cut(source, half, axis, place[d]), cut(target, half, axis, mine), to(d))
            for d in range(1, N)
        ]
        if axis == "b":
            buf[stage + 1, half, mine] = buf[stage, half, mine]
        elif axis == "a":
            buf[stage + 1, half, :, mine] = buf[stage, half, :, mine]
        else:
            buf[stage + 1, half, :, :, mine] = buf[stage, half, :, :, mine]
        return out

    own_mom.wait()
    mb[0] = jnp.zeros((2, N, N, N, 4, LANES), F32)
    for q in range(3):
        for half in range(2):
            part = slice(LANES * half, LANES * (half + 1))
            if q < 2:
                chunk = mom[64 * q : 64 * (q + 1), part]
            else:
                chunk = jnp.concatenate([mom[128:CAP, part], jnp.zeros((32, LANES), F32)])
            eb[q, half, :64] = chunk
            eb[q, half, 64:] = chunk
            for i in range(64):
                mb[0, half, i // 16, (i // 4) % 4, i % 4, q : q + 1, :] = eb[
                    q, half, pl.ds(table_ref[201] + i, 1), :
                ]
    m1 = hop(mb, 0, 0, "z") + hop(mb, 0, 1, "z")
    for d in range(1, N):
        g2a[d - 1].wait_recv()
        g3.append(send(gbuf.at[d, t], gbuf.at[d, t], at_t(1)))
    for d in range(1, N):
        acts_x[d - 1].wait_recv()
        at[0, :, TOK * d : TOK * (d + 1)] = ax[0, d - 1].T
        acts_y[d - 1].wait_recv()
        at[1, :, TOK * d : TOK * (d + 1)] = ax[1, d - 1].T
    for d in range(1, N):
        g2b[d - 1].wait_recv()
        g3.append(send(gbuf.at[d, tt[2]], gbuf.at[d, tt[2]], at_t(1)))
    for c in w1:
        c.wait_recv()
    w2 = []
    for d in range(1, N):
        for j in (2, 3):
            here = wx.at[tt[j], share_x]
            w2.append(send(here, here, at_x(d)))
            here = wx.at[tt[j], share_y]
            w2.append(send(here, here, at_y(d)))
    for c in m1:
        c.wait_recv()
    m2 = hop(mb, 1, 0, "b") + hop(mb, 1, 1, "a")
    for c in g3:
        c.wait_recv()

    first_sums = [None] * N
    order = (0, 2, 1, 3)
    for c in order:
        tile = jnp.dot(
            at[c // 2], gbuf[:, c].reshape(N * TOK, FEAT), preferred_element_type=F32
        )
        for half in range(2):
            part = slice(LANES * half, LANES * (half + 1))
            turned = jnp.swapaxes(tile[:, part].reshape(8, 64, LANES), 0, 1)
            for s in range(64):
                sb[c, (s // 4) % 4, s % 4, s // 16, :, part] = turned[s]
        to, place = (at_y, yz) if c < 2 else (at_x, xs)
        first_sums[c] = [
            send(sb.at[c, place[d]], yr.at[c, d - 1], to(d)) for d in range(1, N)
        ]
    zcopies = [None] * N
    for c in order:
        for copy in first_sums[c]:
            copy.wait_recv()
        ys[c] = (sb[c, y if c < 2 else x] + yr[c, 0]) + (yr[c, 1] + yr[c, 2])
        zcopies[c] = [send(ys.at[c, zs[d]], zr.at[c, d - 1], at_z(d)) for d in range(1, N)]
    for c in w2:
        c.wait_recv()
    w3 = []
    for c in m2:
        c.wait_recv()
    m3 = hop(mb, 2, 0, "a") + hop(mb, 2, 1, "b")
    quarter_y, quarter_x = pl.ds(4 * y, 4), pl.ds(16 + 4 * x, 4)
    for d in range(1, N):
        for j in (2, 3):
            w3.append(send(wx.at[tt[j], quarter_y], wx.at[tt[j], quarter_y], at_y(d)))
            w3.append(send(wx.at[tt[j], quarter_x], wx.at[tt[j], quarter_x], at_x(d)))
    own_rows.wait()
    lane = lax.broadcasted_iota(jnp.int32, (16, 16, FEAT), 1)

    @pl.loop(0, 8)
    def _(i):
        here = pl.ds(pl.multiple_of(16 * i, 16), 16)
        old[here] = jnp.sum(
            jnp.where(lane == lax.rem(stripe, 16), wt[here].astype(F32), 0.0), axis=1
        )

    for c in order:
        for copy in zcopies[c]:
            copy.wait_recv()
        ts[c] = (ys[c, z] + zr[c, 0]) + (zr[c, 1] + zr[c, 2])

    tcopies = [send(ts.at[tt[j]], tr.at[t], at_t(j)) for j in range(1, N)]
    tr[t] = ts[t]
    for c in m3:
        c.wait_recv()
    for half in range(2):
        for i in range(64):
            flat[half, 4 * i : 4 * i + 4, :] = mb[3, half, i // 16, (i // 4) % 4, i % 4]
        for i in range(HELD):
            held[half, i : i + 1, :] = flat[half, pl.ds(table_ref[64 + i], 1), :]
    for c in tcopies:
        c.wait_recv()
    xcopies = [send(tr.at[:, bs[d]], rr.at[:, b], at_b(d)) for d in range(1, N)]
    rr[:, b] = tr[:, b]
    r2[:, 128:, :] = jnp.zeros((2, 8, LANES), F32)
    for c in xcopies:
        c.wait_recv()
    for i in range(N):
        for j in range(N):
            for half in range(2):
                part = slice(LANES * half, LANES * (half + 1))
                r2[half, 32 * i + 8 * j : 32 * i + 8 * j + 8, :] = rr[i, j, :, part]

    total = table_ref[202].astype(F32)
    for half in range(2):
        part = slice(LANES * half, LANES * (half + 1))
        moved = momentum_beta * held[half] + (1.0 - momentum_beta) * (
            r2[half, :HELD, :] / total
        )
        r2[half, :HELD, :] = moved
        soft_sign = moved / jnp.sqrt(moved * moved + soft_eps * soft_eps)
        slots[:, part] = (old[:, part] - learn_rate * soft_sign).astype(BF)

    own_slot = pltpu.make_async_copy(slots, es.at[z, y, x], ls.at[1])
    own_slot.start()
    ez = [send(slots, es.at[z, y, x], at_z(d)) for d in range(1, N)]
    for i in range(N):
        for j in range(N):
            for k in range(N):
                first = table_ref[16 * k + (4 - 3 * h) * j + (1 + 3 * h) * i]
                for half in range(2):
                    pb[0, half, i, j, k] = r2[half, pl.ds(first, 4), :]
    p1 = hop(pb, 0, 0, "b") + hop(pb, 0, 1, "a")

    own_block.wait()
    w1core.wait_recv()
    for c in w3:
        c.wait_recv()
    for n in range(N):
        part = pl.ds(512 * n, 512)
        total = jnp.zeros((TOK, 512), F32)
        for c in range(N):
            total = total + lax.dot_general(
                gbuf[0, c],
                wx[c, 8 * n : 8 * n + 8].reshape(512, FEAT),
                (((1,), (1,)), ((), ())),
                preferred_element_type=F32,
            )
        grads_out[:, part] = total.astype(BF)
    own_grads = pltpu.make_async_copy(grads_out, grads_hbm, ls.at[8])
    own_grads.start()

    own_slot.wait()
    for c in ez:
        c.wait_recv()
    low, high = pl.ds(0, HALF), pl.ds(HALF, HALF)
    near, far = pl.ds(0, 2), pl.ds(2, 2)

    def column(axis, d, zz):
        if axis == "y":
            return es.at[zz, y, lax.rem(x - d + 4, 4), low]
        return es.at[zz, lax.rem(y - d + 4, 4), x, high]

    def passed(axis, d, back, zz):
        if axis == "y":
            return es.at[zz, lax.rem(y - back + 4, 4), lax.rem(x - d + 4, 4), low]
        return es.at[zz, lax.rem(y - d + 4, 4), lax.rem(x - back + 4, 4), high]

    def spread(axis, d):
        to = at_y if axis == "y" else at_x
        out = {}
        for key, zz, step in (("up", near, 1), ("down", far, 3)):
            out[key] = send(column(axis, d, zz), column(axis, d, zz), to(step))
        for key, zz, step in (("up2", far, 1), ("down2", near, 3)):
            out[key] = send(column(axis, d, zz), column(axis, d, zz), to(step))
        return out

    def forward(axis, d, out):
        to = at_y if axis == "y" else at_x
        out["up"].wait_recv()
        here = passed(axis, d, 1, near)
        out["fup"] = send(here, here, to(1))
        out["down"].wait_recv()
        here = passed(axis, d, 3, far)
        out["fdown"] = send(here, here, to(3))

    steps = {
        axis: [
            send(own, own, to(d))
            for to in ((at_x if axis == "y" else at_y),)
            for own in (column(axis, 0, pl.ds(0, 4)),)
            for d in (1, 3, 2)
        ]
        for axis in ("y", "x")
    }
    outs = {axis: [(0, spread(axis, 0))] for axis in ("y", "x")}
    for c in p1:
        c.wait_recv()
    p2 = hop(pb, 1, 0, "a") + hop(pb, 1, 1, "b")
    for i, d in enumerate((1, 3)):
        for axis in ("y", "x"):
            steps[axis][i].wait_recv()
            outs[axis].append((d, spread(axis, d)))
    for axis in ("y", "x"):
        forward(axis, *outs[axis][0])
    for axis in ("y", "x"):
        steps[axis][2].wait_recv()
        outs[axis].append((2, spread(axis, 2)))
    for i in (1, 2, 3):
        for axis in ("y", "x"):
            forward(axis, *outs[axis][i])
        if i == 1:
            for c in p2:
                c.wait_recv()
            p3 = hop(pb, 2, 0, "z") + hop(pb, 2, 1, "z")
    for c in p3:
        c.wait_recv()
    own_keep.wait()
    for half in range(2):
        part = slice(LANES * half, LANES * (half + 1))
        got = pb[3, half].reshape(REPLICAS, 4, LANES)
        for q in range(3):
            eb[q, half, :64] = got[:, q]
            eb[q, half, 64:] = got[:, q]
        rows = jnp.concatenate(
            [eb[q, half, pl.ds(table_ref[200], 64), :] for q in range(3)], axis=0
        )[:CAP]
        kept = keep[:, :LANES].astype(F32)
        new_mom[:, part] = kept * rows + (1.0 - kept) * (
            momentum_beta * mom[:, part]
        )
    for axis in ("y", "x"):
        for _, out in outs[axis]:
            for key in ("up2", "down2", "fup", "fdown"):
                out[key].wait_recv()
    own_grads.wait()
    for c in sent:
        c.wait_send()


N_COPIES = 173


def prepare_kernel(
    rows_ref,
    owner_ref,
    count_ref,
    dv,
    table_ref,
    packed,
):
    me = lax.axis_index("dp")
    h = lax.axis_index("tensor") // 2
    cx, cy = 16 - 12 * h, 4 + 12 * h
    stripe = cx * lax.rem(me, 4) + cy * lax.rem(me // 4, 4) + me // 16

    def step(p, carry):
        start, mine, length, total = carry
        rows, owner = rows_ref[p], owner_ref[p]
        first = (start - stripe + 63) >> 6
        table_ref[owner] = first
        at = cx * (owner & 3) + cy * ((owner >> 2) & 3) + (owner >> 4)
        for q in range(3):
            table_ref[64 + first + q] = 4 * at + q
        here = owner == me
        return (
            start + rows,
            jnp.where(here, start, mine),
            jnp.where(here, rows, length),
            total + count_ref[p],
        )

    zero = jnp.int32(0)
    _, start, length, total = lax.fori_loop(
        0, REPLICAS, step, (zero, zero, zero, zero), unroll=8
    )
    table_ref[200] = lax.rem(start, 64)
    table_ref[201] = 64 - lax.rem(start, 64)
    table_ref[202] = total
    tokens = lax.broadcasted_iota(jnp.int32, (TOK, FEAT), 0)
    packed[:TOK, :] = jnp.where(tokens < count_ref[me], dv[...], jnp.zeros((TOK, FEAT), BF))
    rows = lax.broadcasted_iota(jnp.int32, (CAP, FEAT), 0)
    packed[TOK:, :] = jnp.where(rows < length, 1.0, 0.0).astype(BF)


def place_kernel(
    es, grads, mom, out, grads_out, mom_out, held, rows, passing, moving, in_sem, out_sem, sem
):
    taken = [
        pltpu.make_async_copy(grads, passing, sem.at[0]),
        pltpu.make_async_copy(mom, moving, sem.at[1]),
    ]
    passed = [
        pltpu.make_async_copy(passing, grads_out, sem.at[2]),
        pltpu.make_async_copy(moving, mom_out, sem.at[3]),
    ]
    h = lax.axis_index("tensor") // 2
    steps = HELD // 16
    fetch = [
        pltpu.make_async_copy(
            es.at[:, pl.ds(16 * n, 16)], held.at[:, pl.ds(16 * n, 16)], in_sem.at[n]
        )
        for n in range(steps)
    ]
    for c in fetch + taken:
        c.start()
    row = lax.broadcasted_iota(jnp.int32, (256, 256), 0)
    column = lax.broadcasted_iota(jnp.int32, (256, 256), 1)
    swap = jnp.where(column == 16 * (row & 15) + (row >> 4), 1.0, 0.0).astype(BF)
    store = []
    for n in range(steps):
        here = pl.ds(16 * n, 16)
        fetch[n].wait()
        for c in range(4):
            slabs = jnp.concatenate(
                [
                    held[16 * (i % 4) + (4 - 3 * h) * (i // 4) + (1 + 3 * h) * c, here]
                    for i in range(16)
                ]
            )
            slabs = jnp.dot(swap, slabs, preferred_element_type=F32).astype(BF)
            rows[here, 16 * c : 16 * (c + 1), :] = slabs.reshape(16, 16, FEAT)
        store.append(pltpu.make_async_copy(rows.at[here], out.at[here], out_sem.at[n]))
        store[-1].start()
    for c, d in zip(taken, passed):
        c.wait()
        d.start()
    for c in store + passed:
        c.wait()


def local(acts, dv, w, mom, piece_rows, piece_owner, token_counts):
    smem = pl.BlockSpec(memory_space=pltpu.SMEM)
    vmem = pl.BlockSpec(memory_space=pltpu.VMEM)
    hbm = pl.BlockSpec(memory_space=pl.ANY)
    table, packed = pl.pallas_call(
        prepare_kernel,
        out_shape=(
            jax.ShapeDtypeStruct((208,), jnp.int32),
            jax.ShapeDtypeStruct((TOK + CAP, FEAT), BF),
        ),
        in_specs=[smem, smem, smem, vmem],
        out_specs=(smem, vmem),
    )(piece_rows, piece_owner, token_counts, dv)
    es, new_mom, input_grads = pl.pallas_call(
        exchange_kernel,
        out_shape=(
            jax.ShapeDtypeStruct((N, N, N, HELD, FEAT), BF),
            jax.ShapeDtypeStruct((CAP, FEAT), F32),
            jax.ShapeDtypeStruct((TOK, BLOCK), BF),
        ),
        in_specs=[smem] + [hbm] * 4,
        out_specs=(hbm, vmem, hbm),
        scratch_shapes=[
            pltpu.VMEM((N, N, TOK, FEAT), BF),
            pltpu.VMEM((2, N - 1, TOK, TILE), BF),
            pltpu.VMEM((2, TILE, N * TOK), BF),
            pltpu.VMEM((N, 32, 64, FEAT), BF),
            pltpu.VMEM((N, N, N, N, 8, FEAT), F32),
            pltpu.VMEM((N, N - 1, N, N, 8, FEAT), F32),
            pltpu.VMEM((N, N, N, 8, FEAT), F32),
            pltpu.VMEM((N, N - 1, N, 8, FEAT), F32),
            pltpu.VMEM((N, N, 8, FEAT), F32),
            pltpu.VMEM((N, N, 8, FEAT), F32),
            pltpu.VMEM((N, N, 8, FEAT), F32),
            pltpu.VMEM((2, HELD + 8, LANES), F32),
            pltpu.VMEM((4, 2, N, N, N, 4, LANES), F32),
            pltpu.VMEM((4, 2, N, N, N, 4, LANES), F32),
            pltpu.VMEM((2, 256, LANES), F32),
            pltpu.VMEM((2, HELD, LANES), F32),
            pltpu.VMEM((3, 2, 128, LANES), F32),
            pltpu.VMEM((HELD, 16, FEAT), BF),
            pltpu.VMEM((HELD, FEAT), F32),
            pltpu.VMEM((HELD, FEAT), BF),
            pltpu.VMEM((CAP, FEAT), BF),
            pltpu.VMEM((CAP, FEAT), F32),
            pltpu.VMEM((2, TOK, TILE), BF),
            pltpu.VMEM((TOK, BLOCK), BF),
            pltpu.SemaphoreType.DMA((N_COPIES,)),
            pltpu.SemaphoreType.DMA((N_COPIES,)),
            pltpu.SemaphoreType.DMA((9,)),
        ],
        compiler_params=pltpu.CompilerParams(
            collective_id=0, has_side_effects=True, vmem_limit_bytes=54 * 2**20
        ),
    )(table, acts, packed, mom, w.reshape(ROWS // 64, 64, FEAT))
    new_weight, input_grads, new_mom = pl.pallas_call(
        place_kernel,
        out_shape=(
            jax.ShapeDtypeStruct((HELD, 64, FEAT), BF),
            jax.ShapeDtypeStruct((TOK, BLOCK), BF),
            jax.ShapeDtypeStruct((CAP, FEAT), F32),
        ),
        in_specs=[hbm] * 3,
        out_specs=(hbm, hbm, hbm),
        scratch_shapes=[
            pltpu.VMEM((REPLICAS, HELD, FEAT), BF),
            pltpu.VMEM((HELD, 64, FEAT), BF),
            pltpu.VMEM((TOK, BLOCK), BF),
            pltpu.VMEM((CAP, FEAT), F32),
            pltpu.SemaphoreType.DMA((HELD // 16,)),
            pltpu.SemaphoreType.DMA((HELD // 16,)),
            pltpu.SemaphoreType.DMA((4,)),
        ],
        compiler_params=pltpu.CompilerParams(vmem_limit_bytes=54 * 2**20),
    )(es.reshape(REPLICAS, HELD, FEAT), input_grads, new_mom)
    return input_grads, new_weight.reshape(ROWS, FEAT), new_mom


def solution(mesh):
    return jax.shard_map(
        local,
        mesh=mesh,
        in_specs=(
            P("dp", "tensor"),
            P("dp", "tensor"),
            P(None, "tensor"),
            P("dp", "tensor"),
            P(),
            P(),
            P(),
        ),
        out_specs=(P("dp", "tensor"), P(None, "tensor"), P("dp", "tensor")),
        check_vma=False,
    )
```

```python
import jax
import jax.numpy as jnp
from jax import lax
from jax.experimental import pallas as pl
from jax.experimental.pallas import tpu as pltpu
from jax.sharding import PartitionSpec as P

momentum_beta = 0.9
learn_rate = 0.004
soft_eps = 0.0005

N = 4
REPLICAS = 64
CAP = 160
HELD = 128
HALF = 64
TOK = 256
FEAT = 256
LANES = 128
BLOCK = 2048
TILE = 512
ROWS = 8192
MESH = pl.DeviceIdType.MESH
BF = jnp.bfloat16
F32 = jnp.float32


def exchange_kernel(
    table_ref,
    acts,
    packed,
    mom_in,
    w,
    es,
    new_mom,
    grads_hbm,
    gbuf,
    ax,
    at,
    wx,
    sb,
    yr,
    ys,
    zr,
    ts,
    tr,
    rr,
    r2,
    mb,
    pb,
    flat,
    held,
    eb,
    wt,
    old,
    slots,
    keep,
    mom,
    own,
    grads_out,
    ss,
    rs,
    ls,
):
    me = lax.axis_index("dp")
    t = lax.axis_index("tensor")
    x = lax.rem(me, 4)
    y = lax.rem(me // 4, 4)
    z = me // 16
    xs = [lax.rem(x + d, 4) for d in range(N)]
    yz = [lax.rem(y + d, 4) for d in range(N)]
    zs = [lax.rem(z + d, 4) for d in range(N)]
    h = t // 2
    a = h * x + (1 - h) * y
    b = (1 - h) * x + h * y
    as_ = [lax.rem(a + d, 4) for d in range(N)]
    bs = [lax.rem(b + d, 4) for d in range(N)]
    t1 = t + 1 - 2 * lax.rem(t, 2)
    tt = [t, t1, lax.rem(t + 2, 4), lax.rem(t1 + 2, 4)]

    def at_x(d):
        return (me - x + xs[d], t)

    def at_y(d):
        return (me + 4 * (yz[d] - y), t)

    def at_z(d):
        return (me + 16 * (zs[d] - z), t)

    def at_a(d):
        return (me + h * (xs[d] - x) + (1 - h) * 4 * (yz[d] - y), t)

    def at_b(d):
        return (me + (1 - h) * (xs[d] - x) + h * 4 * (yz[d] - y), t)

    def at_t(j):
        return (me, tt[j])

    partners = [f(d) for f in (at_x, at_y, at_z, at_t) for d in range(1, N)]
    barrier = pltpu.get_barrier_semaphore()
    for p in partners:
        pl.semaphore_signal(barrier, inc=1, device_id=p, device_id_type=MESH)

    n_sem = [0]
    sent = []

    def send(src, dst, to):
        i = n_sem[0]
        n_sem[0] += 1
        c = pltpu.make_async_remote_copy(
            src_ref=src,
            dst_ref=dst,
            send_sem=ss.at[i],
            recv_sem=rs.at[i],
            device_id=to,
            device_id_type=MESH,
        )
        c.start()
        sent.append(c)
        return c

    stripe = 16 * b + 4 * a + z
    own_dv = pltpu.make_async_copy(packed.at[pl.ds(0, TOK)], gbuf.at[0, t], ls.at[5])
    own_dv.start()
    own_acts = [
        pltpu.make_async_copy(acts.at[:, pl.ds(TILE * p, TILE)], own.at[i], ls.at[6 + i])
        for i, p in enumerate((x, y))
    ]
    for c in own_acts:
        c.start()
    own_mom = pltpu.make_async_copy(mom_in, mom, ls.at[4])
    own_mom.start()
    own_keep = pltpu.make_async_copy(packed.at[pl.ds(TOK, CAP)], keep, ls.at[2])
    own_keep.start()
    own_block = pltpu.make_async_copy(w.at[pl.ds(32 * t, 32)], wx.at[t], ls.at[0])
    own_block.start()
    own_rows = pltpu.make_async_copy(
        w.at[:, pl.ds(pl.multiple_of(16 * (stripe // 16), 16), 16)], wt, ls.at[3]
    )
    own_rows.start()

    own_dv.wait()
    pl.semaphore_wait(barrier, len(partners))

    g1 = send(gbuf.at[0, t], gbuf.at[0, t], at_t(2))
    g2a = [send(gbuf.at[0, t], gbuf.at[d, t], at_b(d)) for d in range(1, N)]
    g3 = [send(gbuf.at[0, t], gbuf.at[0, t], at_t(1))]
    acts_x, acts_y = [], []
    for d in range(1, N):
        acts_x.append(send(acts.at[:, pl.ds(TILE * xs[d], TILE)], ax.at[0, d - 1], at_x(d)))
        acts_y.append(send(acts.at[:, pl.ds(TILE * yz[d], TILE)], ax.at[1, d - 1], at_y(d)))
    w1core = send(w.at[pl.ds(32 * t1, 32)], wx.at[t], at_t(1))
    for i in range(2):
        own_acts[i].wait()
        at[i, :, :TOK] = own[i].T
    g1.wait_recv()
    g2b = [send(gbuf.at[0, tt[2]], gbuf.at[d, tt[2]], at_a(d)) for d in range(1, N)]
    g3.append(send(gbuf.at[0, tt[2]], gbuf.at[0, tt[2]], at_t(1)))

    share_x, share_y = 4 * y + x, 16 + 4 * x + y
    w1 = [
        send(w.at[32 * tt[j] + share], wx.at[t, share], at_t(j))
        for j in (2, 3)
        for share in (share_x, share_y)
    ]

    def cut(buf, half, axis, index):
        if axis == "b":
            return buf.at[half, index]
        if axis == "a":
            return buf.at[half, :, index]
        return buf.at[half, :, :, index]

    def hop(buf, stage, half, axis):
        to = {"a": at_a, "b": at_b, "z": at_z}[axis]
        place = {"a": as_, "b": bs, "z": zs}[axis]
        source, target = buf.at[stage], buf.at[stage + 1]
        mine = place[0]
        out = [
            send(cut(source, half, axis, place[d]), cut(target, half, axis, mine), to(d))
            for d in range(1, N)
        ]
        if axis == "b":
            buf[stage + 1, half, mine] = buf[stage, half, mine]
        elif axis == "a":
            buf[stage + 1, half, :, mine] = buf[stage, half, :, mine]
        else:
            buf[stage + 1, half, :, :, mine] = buf[stage, half, :, :, mine]
        return out

    own_mom.wait()
    mb[0] = jnp.zeros((2, N, N, N, 4, LANES), F32)
    for q in range(3):
        for half in range(2):
            part = slice(LANES * half, LANES * (half + 1))
            if q < 2:
                chunk = mom[64 * q : 64 * (q + 1), part]
            else:
                chunk = jnp.concatenate([mom[128:CAP, part], jnp.zeros((32, LANES), F32)])
            eb[q, half, :64] = chunk
            eb[q, half, 64:] = chunk
            for i in range(64):
                mb[0, half, i // 16, (i // 4) % 4, i % 4, q : q + 1, :] = eb[
                    q, half, pl.ds(table_ref[201] + i, 1), :
                ]
    m1 = hop(mb, 0, 0, "z") + hop(mb, 0, 1, "z")
    for d in range(1, N):
        g2a[d - 1].wait_recv()
        g3.append(send(gbuf.at[d, t], gbuf.at[d, t], at_t(1)))
    for d in range(1, N):
        acts_x[d - 1].wait_recv()
        at[0, :, TOK * d : TOK * (d + 1)] = ax[0, d - 1].T
        acts_y[d - 1].wait_recv()
        at[1, :, TOK * d : TOK * (d + 1)] = ax[1, d - 1].T
    for d in range(1, N):
        g2b[d - 1].wait_recv()
        g3.append(send(gbuf.at[d, tt[2]], gbuf.at[d, tt[2]], at_t(1)))
    for c in w1:
        c.wait_recv()
    w2 = []
    for d in range(1, N):
        for j in (2, 3):
            here = wx.at[tt[j], share_x]
            w2.append(send(here, here, at_x(d)))
            here = wx.at[tt[j], share_y]
            w2.append(send(here, here, at_y(d)))
    for c in m1:
        c.wait_recv()
    m2 = hop(mb, 1, 0, "b") + hop(mb, 1, 1, "a")
    for c in g3:
        c.wait_recv()

    first_sums = [None] * N
    order = (0, 2, 1, 3)
    for c in order:
        tile = jnp.dot(
            at[c // 2], gbuf[:, c].reshape(N * TOK, FEAT), preferred_element_type=F32
        )
        for half in range(2):
            part = slice(LANES * half, LANES * (half + 1))
            turned = jnp.swapaxes(tile[:, part].reshape(8, 64, LANES), 0, 1)
            for s in range(64):
                sb[c, (s // 4) % 4, s % 4, s // 16, :, part] = turned[s]
        to, place = (at_y, yz) if c < 2 else (at_x, xs)
        first_sums[c] = [
            send(sb.at[c, place[d]], yr.at[c, d - 1], to(d)) for d in range(1, N)
        ]
    zcopies = [None] * N
    for c in order:
        for copy in first_sums[c]:
            copy.wait_recv()
        ys[c] = (sb[c, y if c < 2 else x] + yr[c, 0]) + (yr[c, 1] + yr[c, 2])
        zcopies[c] = [send(ys.at[c, zs[d]], zr.at[c, d - 1], at_z(d)) for d in range(1, N)]
    for c in w2:
        c.wait_recv()
    w3 = []
    for c in m2:
        c.wait_recv()
    m3 = hop(mb, 2, 0, "a") + hop(mb, 2, 1, "b")
    quarter_y, quarter_x = pl.ds(4 * y, 4), pl.ds(16 + 4 * x, 4)

    def last_share(j):
        for d in range(1, N):
            w3.append(send(wx.at[tt[j], quarter_y], wx.at[tt[j], quarter_y], at_y(d)))
            w3.append(send(wx.at[tt[j], quarter_x], wx.at[tt[j], quarter_x], at_x(d)))

    last_share(2)
    own_rows.wait()
    lane = lax.broadcasted_iota(jnp.int32, (16, 16, FEAT), 1)

    @pl.loop(0, 8)
    def _(i):
        here = pl.ds(pl.multiple_of(16 * i, 16), 16)
        old[here] = jnp.sum(
            jnp.where(lane == lax.rem(stripe, 16), wt[here].astype(F32), 0.0), axis=1
        )

    for c in order:
        for copy in zcopies[c]:
            copy.wait_recv()
        ts[c] = (ys[c, z] + zr[c, 0]) + (zr[c, 1] + zr[c, 2])

    tcopies = [send(ts.at[tt[j]], tr.at[t], at_t(j)) for j in range(1, N)]
    tr[t] = ts[t]
    for c in m3:
        c.wait_recv()
    for half in range(2):
        for i in range(64):
            flat[half, 4 * i : 4 * i + 4, :] = mb[3, half, i // 16, (i // 4) % 4, i % 4]
        for i in range(HELD):
            held[half, i : i + 1, :] = flat[half, pl.ds(table_ref[64 + i], 1), :]
    for c in tcopies:
        c.wait_recv()
    xcopies = [send(tr.at[:, bs[d]], rr.at[:, b], at_b(d)) for d in range(1, N)]
    last_share(3)
    rr[:, b] = tr[:, b]
    r2[:, 128:, :] = jnp.zeros((2, 8, LANES), F32)
    for c in xcopies:
        c.wait_recv()
    for i in range(N):
        for j in range(N):
            for half in range(2):
                part = slice(LANES * half, LANES * (half + 1))
                r2[half, 32 * i + 8 * j : 32 * i + 8 * j + 8, :] = rr[i, j, :, part]

    total = table_ref[202].astype(F32)
    for half in range(2):
        part = slice(LANES * half, LANES * (half + 1))
        moved = momentum_beta * held[half] + (1.0 - momentum_beta) * (
            r2[half, :HELD, :] / total
        )
        r2[half, :HELD, :] = moved
        soft_sign = moved / jnp.sqrt(moved * moved + soft_eps * soft_eps)
        slots[:, part] = (old[:, part] - learn_rate * soft_sign).astype(BF)

    own_slot = pltpu.make_async_copy(slots, es.at[z, y, x], ls.at[1])
    own_slot.start()
    ez = [send(slots, es.at[z, y, x], at_z(d)) for d in range(1, N)]
    for i in range(N):
        for j in range(N):
            for k in range(N):
                first = table_ref[16 * k + (4 - 3 * h) * j + (1 + 3 * h) * i]
                for half in range(2):
                    pb[0, half, i, j, k] = r2[half, pl.ds(first, 4), :]
    p1 = hop(pb, 0, 0, "b") + hop(pb, 0, 1, "a")

    own_slot.wait()
    for c in ez:
        c.wait_recv()
    low, high = pl.ds(0, HALF), pl.ds(HALF, HALF)
    near, far = pl.ds(0, 2), pl.ds(2, 2)

    def column(axis, d, zz):
        if axis == "y":
            return es.at[zz, y, lax.rem(x - d + 4, 4), low]
        return es.at[zz, lax.rem(y - d + 4, 4), x, high]

    def passed(axis, d, back, zz):
        if axis == "y":
            return es.at[zz, lax.rem(y - back + 4, 4), lax.rem(x - d + 4, 4), low]
        return es.at[zz, lax.rem(y - d + 4, 4), lax.rem(x - back + 4, 4), high]

    def spread(axis, d):
        to = at_y if axis == "y" else at_x
        out = {}
        for key, zz, step in (("up", near, 1), ("down", far, 3)):
            out[key] = send(column(axis, d, zz), column(axis, d, zz), to(step))
        for key, zz, step in (("up2", far, 1), ("down2", near, 3)):
            out[key] = send(column(axis, d, zz), column(axis, d, zz), to(step))
        return out

    def forward(axis, d, out):
        to = at_y if axis == "y" else at_x
        out["up"].wait_recv()
        here = passed(axis, d, 1, near)
        out["fup"] = send(here, here, to(1))
        out["down"].wait_recv()
        here = passed(axis, d, 3, far)
        out["fdown"] = send(here, here, to(3))

    steps = {
        axis: [
            send(own, own, to(d))
            for to in ((at_x if axis == "y" else at_y),)
            for own in (column(axis, 0, pl.ds(0, 4)),)
            for d in (1, 3, 2)
        ]
        for axis in ("y", "x")
    }
    outs = {axis: [(0, spread(axis, 0))] for axis in ("y", "x")}

    own_block.wait()
    w1core.wait_recv()
    for c in w3:
        c.wait_recv()
    for n in range(N):
        part = pl.ds(512 * n, 512)
        total = jnp.zeros((TOK, 512), F32)
        for c in range(N):
            total = total + lax.dot_general(
                gbuf[0, c],
                wx[c, 8 * n : 8 * n + 8].reshape(512, FEAT),
                (((1,), (1,)), ((), ())),
                preferred_element_type=F32,
            )
        grads_out[:, part] = total.astype(BF)
    own_grads = pltpu.make_async_copy(grads_out, grads_hbm, ls.at[8])
    own_grads.start()

    for c in p1:
        c.wait_recv()
    p2 = hop(pb, 1, 0, "a") + hop(pb, 1, 1, "b")
    for i, d in enumerate((1, 3)):
        for axis in ("y", "x"):
            steps[axis][i].wait_recv()
            outs[axis].append((d, spread(axis, d)))
    for axis in ("y", "x"):
        forward(axis, *outs[axis][0])
    for axis in ("y", "x"):
        steps[axis][2].wait_recv()
        outs[axis].append((2, spread(axis, 2)))
    for i in (1, 2, 3):
        for axis in ("y", "x"):
            forward(axis, *outs[axis][i])
        if i == 1:
            for c in p2:
                c.wait_recv()
            p3 = hop(pb, 2, 0, "z") + hop(pb, 2, 1, "z")
    for c in p3:
        c.wait_recv()
    own_keep.wait()
    for half in range(2):
        part = slice(LANES * half, LANES * (half + 1))
        got = pb[3, half].reshape(REPLICAS, 4, LANES)
        for q in range(3):
            eb[q, half, :64] = got[:, q]
            eb[q, half, 64:] = got[:, q]
        rows = jnp.concatenate(
            [eb[q, half, pl.ds(table_ref[200], 64), :] for q in range(3)], axis=0
        )[:CAP]
        kept = keep[:, :LANES].astype(F32)
        new_mom[:, part] = kept * rows + (1.0 - kept) * (
            momentum_beta * mom[:, part]
        )
    for axis in ("y", "x"):
        for _, out in outs[axis]:
            for key in ("up2", "down2", "fup", "fdown"):
                out[key].wait_recv()
    own_grads.wait()
    for c in sent:
        c.wait_send()


N_COPIES = 173


def prepare_kernel(
    rows_ref,
    owner_ref,
    count_ref,
    dv,
    table_ref,
    packed,
):
    me = lax.axis_index("dp")
    h = lax.axis_index("tensor") // 2
    cx, cy = 16 - 12 * h, 4 + 12 * h
    stripe = cx * lax.rem(me, 4) + cy * lax.rem(me // 4, 4) + me // 16

    def step(p, carry):
        start, mine, length, total = carry
        rows, owner = rows_ref[p], owner_ref[p]
        first = (start - stripe + 63) >> 6
        table_ref[owner] = first
        at = cx * (owner & 3) + cy * ((owner >> 2) & 3) + (owner >> 4)
        for q in range(3):
            table_ref[64 + first + q] = 4 * at + q
        here = owner == me
        return (
            start + rows,
            jnp.where(here, start, mine),
            jnp.where(here, rows, length),
            total + count_ref[p],
        )

    zero = jnp.int32(0)
    _, start, length, total = lax.fori_loop(
        0, REPLICAS, step, (zero, zero, zero, zero), unroll=8
    )
    table_ref[200] = lax.rem(start, 64)
    table_ref[201] = 64 - lax.rem(start, 64)
    table_ref[202] = total
    tokens = lax.broadcasted_iota(jnp.int32, (TOK, FEAT), 0)
    packed[:TOK, :] = jnp.where(tokens < count_ref[me], dv[...], jnp.zeros((TOK, FEAT), BF))
    rows = lax.broadcasted_iota(jnp.int32, (CAP, FEAT), 0)
    packed[TOK:, :] = jnp.where(rows < length, 1.0, 0.0).astype(BF)


def place_kernel(
    es, grads, mom, out, grads_out, mom_out, held, rows, passing, moving, in_sem, out_sem, sem
):
    taken = [
        pltpu.make_async_copy(grads, passing, sem.at[0]),
        pltpu.make_async_copy(mom, moving, sem.at[1]),
    ]
    passed = [
        pltpu.make_async_copy(passing, grads_out, sem.at[2]),
        pltpu.make_async_copy(moving, mom_out, sem.at[3]),
    ]
    h = lax.axis_index("tensor") // 2
    steps = HELD // 16
    fetch = [
        pltpu.make_async_copy(
            es.at[:, pl.ds(16 * n, 16)], held.at[:, pl.ds(16 * n, 16)], in_sem.at[n]
        )
        for n in range(steps)
    ]
    for c in fetch + taken:
        c.start()
    row = lax.broadcasted_iota(jnp.int32, (256, 256), 0)
    column = lax.broadcasted_iota(jnp.int32, (256, 256), 1)
    swap = jnp.where(column == 16 * (row & 15) + (row >> 4), 1.0, 0.0).astype(BF)
    store = []
    for n in range(steps):
        here = pl.ds(16 * n, 16)
        fetch[n].wait()
        for c in range(4):
            slabs = jnp.concatenate(
                [
                    held[16 * (i % 4) + (4 - 3 * h) * (i // 4) + (1 + 3 * h) * c, here]
                    for i in range(16)
                ]
            )
            slabs = jnp.dot(swap, slabs, preferred_element_type=F32).astype(BF)
            rows[here, 16 * c : 16 * (c + 1), :] = slabs.reshape(16, 16, FEAT)
        store.append(pltpu.make_async_copy(rows.at[here], out.at[here], out_sem.at[n]))
        store[-1].start()
    for c, d in zip(taken, passed):
        c.wait()
        d.start()
    for c in store + passed:
        c.wait()


def local(acts, dv, w, mom, piece_rows, piece_owner, token_counts):
    smem = pl.BlockSpec(memory_space=pltpu.SMEM)
    vmem = pl.BlockSpec(memory_space=pltpu.VMEM)
    hbm = pl.BlockSpec(memory_space=pl.ANY)
    table, packed = pl.pallas_call(
        prepare_kernel,
        out_shape=(
            jax.ShapeDtypeStruct((208,), jnp.int32),
            jax.ShapeDtypeStruct((TOK + CAP, FEAT), BF),
        ),
        in_specs=[smem, smem, smem, vmem],
        out_specs=(smem, vmem),
    )(piece_rows, piece_owner, token_counts, dv)
    es, new_mom, input_grads = pl.pallas_call(
        exchange_kernel,
        out_shape=(
            jax.ShapeDtypeStruct((N, N, N, HELD, FEAT), BF),
            jax.ShapeDtypeStruct((CAP, FEAT), F32),
            jax.ShapeDtypeStruct((TOK, BLOCK), BF),
        ),
        in_specs=[smem] + [hbm] * 4,
        out_specs=(hbm, vmem, hbm),
        scratch_shapes=[
            pltpu.VMEM((N, N, TOK, FEAT), BF),
            pltpu.VMEM((2, N - 1, TOK, TILE), BF),
            pltpu.VMEM((2, TILE, N * TOK), BF),
            pltpu.VMEM((N, 32, 64, FEAT), BF),
            pltpu.VMEM((N, N, N, N, 8, FEAT), F32),
            pltpu.VMEM((N, N - 1, N, N, 8, FEAT), F32),
            pltpu.VMEM((N, N, N, 8, FEAT), F32),
            pltpu.VMEM((N, N - 1, N, 8, FEAT), F32),
            pltpu.VMEM((N, N, 8, FEAT), F32),
            pltpu.VMEM((N, N, 8, FEAT), F32),
            pltpu.VMEM((N, N, 8, FEAT), F32),
            pltpu.VMEM((2, HELD + 8, LANES), F32),
            pltpu.VMEM((4, 2, N, N, N, 4, LANES), F32),
            pltpu.VMEM((4, 2, N, N, N, 4, LANES), F32),
            pltpu.VMEM((2, 256, LANES), F32),
            pltpu.VMEM((2, HELD, LANES), F32),
            pltpu.VMEM((3, 2, 128, LANES), F32),
            pltpu.VMEM((HELD, 16, FEAT), BF),
            pltpu.VMEM((HELD, FEAT), F32),
            pltpu.VMEM((HELD, FEAT), BF),
            pltpu.VMEM((CAP, FEAT), BF),
            pltpu.VMEM((CAP, FEAT), F32),
            pltpu.VMEM((2, TOK, TILE), BF),
            pltpu.VMEM((TOK, BLOCK), BF),
            pltpu.SemaphoreType.DMA((N_COPIES,)),
            pltpu.SemaphoreType.DMA((N_COPIES,)),
            pltpu.SemaphoreType.DMA((9,)),
        ],
        compiler_params=pltpu.CompilerParams(
            collective_id=0, has_side_effects=True, vmem_limit_bytes=54 * 2**20
        ),
    )(table, acts, packed, mom, w.reshape(ROWS // 64, 64, FEAT))
    new_weight, input_grads, new_mom = pl.pallas_call(
        place_kernel,
        out_shape=(
            jax.ShapeDtypeStruct((HELD, 64, FEAT), BF),
            jax.ShapeDtypeStruct((TOK, BLOCK), BF),
            jax.ShapeDtypeStruct((CAP, FEAT), F32),
        ),
        in_specs=[hbm] * 3,
        out_specs=(hbm, hbm, hbm),
        scratch_shapes=[
            pltpu.VMEM((REPLICAS, HELD, FEAT), BF),
            pltpu.VMEM((HELD, 64, FEAT), BF),
            pltpu.VMEM((TOK, BLOCK), BF),
            pltpu.VMEM((CAP, FEAT), F32),
            pltpu.SemaphoreType.DMA((HELD // 16,)),
            pltpu.SemaphoreType.DMA((HELD // 16,)),
            pltpu.SemaphoreType.DMA((4,)),
        ],
        compiler_params=pltpu.CompilerParams(vmem_limit_bytes=54 * 2**20),
    )(es.reshape(REPLICAS, HELD, FEAT), input_grads, new_mom)
    return input_grads, new_weight.reshape(ROWS, FEAT), new_mom


def solution(mesh):
    return jax.shard_map(
        local,
        mesh=mesh,
        in_specs=(
            P("dp", "tensor"),
            P("dp", "tensor"),
            P(None, "tensor"),
            P("dp", "tensor"),
            P(),
            P(),
            P(),
        ),
        out_specs=(P("dp", "tensor"), P(None, "tensor"), P("dp", "tensor")),
        check_vma=False,
    )
```
